128 devices in a mesh: group: 8 (over z, core), mp: 16 (over x, y).
Axes of the slice: x: 4, y: 4, z: 4, core: 2. Of those that a mesh axis runs over, the one named last changes fastest.
Arguments:
- tokens: bfloat16 [1024, 16384], P('group', 'mp'), may hold values from -6 to 6
- gate_weight: bfloat16 [16384, 26624], P('mp', 'group'), may hold values from -0.046875 to 0.046875
- up_weight: bfloat16 [16384, 26624], P('mp', 'group'), may hold values from -0.046875 to 0.046875
- down_weight: bfloat16 [26624, 16384], P('group', 'mp'), may hold values from -0.0390625 to 0.0390625
Outputs:
- mixed: bfloat16 [1024, 16384], P('group', 'mp')
The draws below stay inside these ranges and needn't reach their ends.
All inputs are finite; a program needn't handle non-finite values.
Results may differ from the reference program's by a relative error of at most 0.034.
Values may be sent and summed in bfloat16 or wider, within the bound.
No kernel may reach another device: no remote copies, remote signals or barrier semaphores. Data moves between devices by JAX's collectives and lax.ppermute only.
A program may use at most 128 MiB of HBM per device.

```python
import jax
import jax.numpy as jnp
from jax import lax

D = 16384
FF = 26624
TOKENS = 1024
N_MP = 16


def steps_of(stream_key, dims, pieces, smallest, largest):
    factor_of, own = 1.0, jax.random.fold_in(stream_key, 6)
    for axis_at, blocks in pieces:
        steps = jnp.exp(jax.random.uniform(jax.random.fold_in(own, axis_at), (blocks,), jnp.float32, smallest / len(pieces), largest / len(pieces)))
        factor_of = factor_of * jnp.repeat(steps, dims[axis_at] // blocks).reshape([-1 if axis == axis_at else 1 for axis in range(len(dims))])
    return factor_of


def bell_draw(key, shape, deviation, reach, pieces=(), held_as=jnp.bfloat16):
    result = jax.random.normal(key, shape, jnp.float32) * deviation
    if len(pieces) > 0:
        result = steps_of(key, shape, pieces, -0.22, 0.18) * result
    return jnp.clip(result, min=-reach, max=reach).astype(held_as)


def setup_inputs(seed: int = 0) -> dict:
    streams_of = jax.random.split(jax.random.key(seed), 5)
    return {
        "tokens": bell_draw(streams_of[0], (TOKENS, D), 1.0, 6.0, ((0, 8), (1, 16))),
        "gate_weight": bell_draw(streams_of[1], (D, FF), D ** -0.5, 0.046875, ((0, 16), (1, 8))),
        "up_weight": bell_draw(streams_of[2], (D, FF), D ** -0.5, 0.046875, ((0, 16), (1, 8))),
        "down_weight": bell_draw(streams_of[3], (FF, D), FF ** -0.5, 0.0390625, ((0, 8), (1, 16))),
    }


def reference(tokens, gate_weight, up_weight, down_weight):
    width_block = D // N_MP

    def add_block(carry, index):
        first_row = (index * width_block).astype(jnp.int32)
        token_cols = lax.dynamic_slice_in_dim(tokens, first_row, width_block, 1)
        gate_rows = lax.dynamic_slice_in_dim(gate_weight, first_row, width_block, 0)
        up_rows = lax.dynamic_slice_in_dim(up_weight, first_row, width_block, 0)
        gate_part = jnp.dot(token_cols, gate_rows, preferred_element_type=jnp.float32).astype(jnp.bfloat16)
        up_part = jnp.dot(token_cols, up_rows, preferred_element_type=jnp.float32).astype(jnp.bfloat16)
        gate_part, up_part = lax.optimization_barrier((gate_part, up_part))
        return (carry[0] + gate_part.astype(jnp.float32), carry[1] + up_part.astype(jnp.float32)), None

    zeros_init = jnp.zeros((TOKENS, FF), jnp.float32)
    (gate, up_sum), _ = lax.scan(add_block, (zeros_init, zeros_init), jnp.arange(N_MP, dtype=jnp.int32))
    hidden = (jax.nn.silu(gate) * up_sum).astype(jnp.bfloat16)
    return jnp.dot(hidden, down_weight, preferred_element_type=jnp.float32).astype(jnp.bfloat16)
```

```python
import jax
import jax.numpy as jnp
from jax import lax
from jax.sharding import PartitionSpec as P


def local(tokens, gate_weight, up_weight, down_weight):
    rows = lax.all_gather(tokens, "group", axis=0, tiled=True)
    gate_part = jnp.dot(rows, gate_weight, preferred_element_type=jnp.float32).astype(jnp.bfloat16)
    up_part = jnp.dot(rows, up_weight, preferred_element_type=jnp.float32).astype(jnp.bfloat16)
    gate = lax.psum_scatter(gate_part, "mp", scatter_dimension=0, tiled=True).astype(jnp.float32)
    up = lax.psum_scatter(up_part, "mp", scatter_dimension=0, tiled=True).astype(jnp.float32)
    hidden = (jax.nn.silu(gate) * up).astype(jnp.bfloat16)
    hidden = lax.all_gather(hidden, "mp", axis=0, tiled=True)
    down = jnp.dot(hidden, down_weight, preferred_element_type=jnp.float32).astype(jnp.bfloat16)
    return lax.psum_scatter(down, "group", scatter_dimension=0, tiled=True)


def solution(mesh):
    placed = (P("group", "mp"), P("mp", "group"), P("mp", "group"), P("group", "mp"))
    return jax.shard_map(
        local, mesh=mesh, in_specs=placed, out_specs=P("group", "mp"), check_vma=False
    )
```

```python
import functools

import jax
import jax.numpy as jnp
import numpy as np
from jax import lax
from jax.experimental import pallas as pl
from jax.experimental.pallas import tpu as pltpu
from jax.sharding import PartitionSpec as P

BF = jnp.bfloat16
F32 = jnp.float32

PAIR = {"e": (1, 0, 3, 2), "o": (3, 2, 1, 0)}
BIT = {"e": (0, 1, 1, 0), "o": (0, 0, 1, 1)}
ORDERS = (
    (("x", "e"), ("x", "o"), ("y", "e"), ("y", "o")),
    (("x", "o"), ("x", "e"), ("y", "o"), ("y", "e")),
), (
    (("y", "e"), ("y", "o"), ("x", "e"), ("x", "o")),
    (("y", "o"), ("y", "e"), ("x", "o"), ("x", "e")),
)


def partner(m, link):
    axis, kind = link
    x, y = divmod(m, 4)
    return 4 * PAIR[kind][x] + y if axis == "x" else 4 * x + PAIR[kind][y]


def bit_of(m, link):
    axis, kind = link
    x, y = divmod(m, 4)
    return BIT[kind][x if axis == "x" else y]


def pairs_of(flow, step):
    return [
        (g * 16 + m, g * 16 + partner(m, ORDERS[g % 2][flow][step]))
        for g in range(8)
        for m in range(16)
    ]


def mask_table():
    table = np.zeros((2, 2, 16), np.int32)
    for core in range(2):
        for flow in range(2):
            for m in range(16):
                own = 0
                for link in ORDERS[core][flow]:
                    own = 2 * own + bit_of(m, link)
                table[core, flow, m] = 15 ^ own
    return table


def group_pairs(shift):
    return [(g, (g + 2 * shift) % 8) for g in range(8)]


SWAP = [(g, g ^ 1) for g in range(8)]


def swap(a):
    return lax.ppermute(a, "group", SWAP)


def exchange(a, flow, step):
    return lax.ppermute(a, ("group", "mp"), pairs_of(flow, step))


def project_body(info, t0, s0, t1, s1, gate, up, send, keep, plain, turned):
    @pl.when(pl.program_id(0) == 0)
    def _():
        half = t0.shape[0]
        for t, (mine, other) in enumerate(((t0, s0), (t1, s1))):
            plain[pl.ds(2 * t * half, half)] = mine[...]
            plain[pl.ds((2 * t + 1) * half, half)] = other[...]
        for t in range(2):
            for r in range(16):
                source = pl.multiple_of(t * 256 + (r ^ info[0]) * 16, 16)
                turned[pl.ds(t * 256 + r * 16, 16)] = plain[pl.ds(source, 16)]

    both = jnp.concatenate((gate[...], up[...]), axis=1)
    res = jnp.dot(turned[...], both, preferred_element_type=F32).astype(BF)
    for t in range(2):
        for k in range(2):
            part = res[t * 256 : (t + 1) * 256, k * 128 : (k + 1) * 128]
            send[k, t] = part[:128]
            keep[k, t] = part[128:]


def project(info, tokens, gate, up, columns):
    tiles = columns // 128
    whole = pl.BlockSpec((128, 1024), lambda j, info: (0, 0))
    weight = pl.BlockSpec((1024, 128), lambda j, info: (0, info[1] + j))
    out = pl.BlockSpec((2, 2, 128, 128), lambda j, info: (0, 0, 0, j))
    shape = jax.ShapeDtypeStruct((2, 2, 128, columns), BF)
    return pl.pallas_call(
        project_body,
        grid_spec=pltpu.PrefetchScalarGridSpec(
            num_scalar_prefetch=1,
            grid=(tiles,),
            in_specs=[whole] * 4 + [weight] * 2,
            out_specs=[out] * 2,
            scratch_shapes=[pltpu.VMEM((512, 1024), BF)] * 2,
        ),
        out_shape=[shape] * 2,
        compiler_params=pltpu.CompilerParams(vmem_limit_bytes=24 << 20),
        cost_estimate=pl.CostEstimate(
            flops=2 * 512 * 1024 * 2 * columns, bytes_accessed=12 << 20, transcendentals=0
        ),
        name="project",
    )(info, *tokens, gate, up)


def down_tile(theirs, mine, weight):
    rows = jnp.concatenate((theirs[0], mine[0], theirs[1], mine[1]), axis=0)
    return jnp.dot(rows, weight[...], preferred_element_type=F32)


def down_first_body(info, theirs, mine, weight, out):
    res = down_tile(theirs, mine, weight)
    for t in range(2):
        for r in range(16):
            target = pl.multiple_of((r ^ info[0]) * 16, 16)
            out[t, pl.ds(target, 16)] = res[t * 256 + r * 16 : t * 256 + (r + 1) * 16]


def down_last_body(info, theirs, mine, weight, before, send, keep, turned):
    res = down_tile(theirs, mine, weight)
    for t in range(2):
        for r in range(16):
            target = pl.multiple_of((r ^ info[0]) * 16, 16)
            turned[t, pl.ds(target, 16)] = res[t * 256 + r * 16 : t * 256 + (r + 1) * 16]
    total = turned[...] + before[...]
    keep[...] = total[:, :128]
    send[...] = total[:, 128:].astype(BF)


def down(info, theirs, mine, weight, before=None):
    depth = theirs.shape[2]
    wide = 256
    hidden = pl.BlockSpec((2, 128, depth), lambda j, info: (0, 0, 0))
    weights = pl.BlockSpec((depth, wide), lambda j, info: (info[1], j))
    total = pl.BlockSpec((2, 256, wide), lambda j, info: (0, 0, j))
    half = pl.BlockSpec((2, 128, wide), lambda j, info: (0, 0, j))
    first = before is None
    return pl.pallas_call(
        down_first_body if first else down_last_body,
        grid_spec=pltpu.PrefetchScalarGridSpec(
            num_scalar_prefetch=1,
            grid=(1024 // wide,),
            in_specs=[hidden, hidden, weights] + ([] if first else [total]),
            out_specs=total if first else [half, half],
            scratch_shapes=[] if first else [pltpu.VMEM((2, 256, wide), F32)],
        ),
        out_shape=jax.ShapeDtypeStruct((2, 256, 1024), F32)
        if first
        else [
            jax.ShapeDtypeStruct((2, 128, 1024), BF),
            jax.ShapeDtypeStruct((2, 128, 1024), F32),
        ],
        compiler_params=pltpu.CompilerParams(vmem_limit_bytes=24 << 20),
        cost_estimate=pl.CostEstimate(
            flops=2 * 512 * 1024 * depth, bytes_accessed=7 << 20, transcendentals=0
        ),
        name="down",
    )(info, theirs, mine, weight, *(() if first else (before,)))


def add(a, b):
    return (a.astype(F32) + b.astype(F32)).astype(BF)


def reduce_and_gather(send, keep, flow):
    for step in range(3):
        came = exchange(send, flow, step)
        half = keep.shape[2] // 2
        send = add(keep[:, :, :half], came[:, :, :half])
        keep = add(keep[:, :, half:], came[:, :, half:])
    came = exchange(send, flow, 3)
    total = keep.astype(F32) + came.astype(F32)
    mine = (jax.nn.silu(total[0]) * total[1]).astype(BF)
    for step in (3, 2, 1):
        theirs = exchange(mine, flow, step)
        mine = jnp.concatenate((theirs, mine), axis=1)
    return exchange(mine, flow, 0), mine


def local(tokens, gate_weight, up_weight, down_weight):
    core = lax.axis_index("group") % 2
    masks = jnp.asarray(mask_table())[core, :, lax.axis_index("mp")]
    columns = gate_weight.shape[1] // 2

    def info(flow, offset):
        return jnp.stack((masks[flow], jnp.asarray(offset, jnp.int32)))

    def fetch(shift):
        return lax.ppermute(tokens, "group", group_pairs(-shift))

    opposite, after, before = fetch(2), fetch(1), fetch(-1)
    pair_a = (tokens, swap(tokens), opposite, swap(opposite))
    pair_b = (after, swap(after), before, swap(before))

    given = (1 - core) * columns
    gate_other = swap(lax.dynamic_slice_in_dim(gate_weight, given, columns, 1))
    up_other = swap(lax.dynamic_slice_in_dim(up_weight, given, columns, 1))
    down_other = swap(lax.dynamic_slice_in_dim(down_weight, given, columns, 0))

    def unit(pair, flow, own):
        if own:
            send, keep = project(
                info(flow, core * (columns // 128)), pair, gate_weight, up_weight, columns
            )
        else:
            send, keep = project(info(flow, 0), pair, gate_other, up_other, columns)
        return reduce_and_gather(send, keep, flow)

    a_own = unit(pair_a, 0, True)
    b_own = unit(pair_b, 1, True)
    a_other = unit(pair_a, 0, False)
    b_other = unit(pair_b, 1, False)

    a_half = down(info(0, core), *a_own, down_weight)
    b_half = down(info(1, core), *b_own, down_weight)
    a_send, a_keep = down(info(0, 0), *a_other, down_other, a_half)
    b_send, b_keep = down(info(1, 0), *b_other, down_other, b_half)

    a_total = a_keep + swap(a_send).astype(F32)
    b_total = b_keep + swap(b_send).astype(F32)
    from_opposite = lax.ppermute(a_total[1].astype(BF), "group", group_pairs(2))
    from_before = lax.ppermute(b_total[0].astype(BF), "group", group_pairs(1))
    from_after = lax.ppermute(b_total[1].astype(BF), "group", group_pairs(-1))
    total = a_total[0] + from_opposite.astype(F32)
    total = total + from_before.astype(F32) + from_after.astype(F32)
    return total.astype(BF)


def solution(mesh):
    placed = (P("group", "mp"), P("mp", "group"), P("mp", "group"), P("group", "mp"))
    return jax.shard_map(
        local, mesh=mesh, in_specs=placed, out_specs=P("group", "mp"), check_vma=False
    )
```

```python
import functools

import jax
import jax.numpy as jnp
import numpy as np
from jax import lax
from jax.experimental import pallas as pl
from jax.experimental.pallas import tpu as pltpu
from jax.sharding import PartitionSpec as P

BF = jnp.bfloat16
F32 = jnp.float32
COST = 1000

PAIR = {"e": (1, 0, 3, 2), "o": (3, 2, 1, 0)}
BIT = {"e": (0, 1, 1, 0), "o": (0, 0, 1, 1)}
ORDERS = (
    (("x", "e"), ("x", "o"), ("y", "e"), ("y", "o")),
    (("x", "o"), ("x", "e"), ("y", "o"), ("y", "e")),
), (
    (("y", "e"), ("y", "o"), ("x", "e"), ("x", "o")),
    (("y", "o"), ("y", "e"), ("x", "o"), ("x", "e")),
)


def partner(m, link):
    axis, kind = link
    x, y = divmod(m, 4)
    return 4 * PAIR[kind][x] + y if axis == "x" else 4 * x + PAIR[kind][y]


def bit_of(m, link):
    axis, kind = link
    x, y = divmod(m, 4)
    return BIT[kind][x if axis == "x" else y]


def pairs_of(flow, step):
    return [
        (g * 16 + m, g * 16 + partner(m, ORDERS[g % 2][flow][step]))
        for g in range(8)
        for m in range(16)
    ]


def mask_table():
    table = np.zeros((2, 2, 16), np.int32)
    for core in range(2):
        for flow in range(2):
            for m in range(16):
                own = 0
                for link in ORDERS[core][flow]:
                    own = 2 * own + bit_of(m, link)
                table[core, flow, m] = 15 ^ own
    return table


def group_pairs(shift):
    return [(g, (g + 2 * shift) % 8) for g in range(8)]


SWAP = [(g, g ^ 1) for g in range(8)]


def swap(a):
    return lax.ppermute(a, "group", SWAP)


def exchange(a, flow, step):
    return lax.ppermute(a, ("group", "mp"), pairs_of(flow, step))


CHUNKS = ((0, 512), (512, 512), (1024, 640))


def project_body(sizes, info, *refs):
    count = 2 * len(sizes)
    blocks = refs[:count]
    gate, up = refs[count : count + 2]
    send, keep, plain, turned, weights, staged, in_sem, out_sem = refs[-8:]
    pairs = sum(sizes)
    offset = pl.multiple_of(info[1], 128)

    def fetch(k, c):
        start, width = CHUNKS[c]
        source = (gate, up)[k].at[:, pl.ds(pl.multiple_of(offset + start, 128), width)]
        return pltpu.make_async_copy(
            source, weights.at[k, :, pl.ds(start, width)], in_sem.at[k, c]
        )

    def put(k, c, which):
        start, width = CHUNKS[c]
        source = staged.at[k, :, pl.ds(which * 128, 128), pl.ds(start, width)]
        target = (send, keep)[which].at[k, :, :, pl.ds(start, width)]
        return pltpu.make_async_copy(source, target, out_sem.at[k, c, which])

    for c in range(2):
        for k in range(2):
            fetch(k, c).start()

    at = 0
    for i, size in enumerate(sizes):
        for t in range(size):
            plain[pl.ds(at, 128)] = blocks[2 * i][t]
            plain[pl.ds(at + 128, 128)] = blocks[2 * i + 1][t]
            at += 256
    for t in range(pairs):
        for r in range(16):
            source = pl.multiple_of(t * 256 + (r ^ info[0]) * 16, 16)
            turned[pl.ds(t * 256 + r * 16, 16)] = plain[pl.ds(source, 16)]

    def tile(k, at):
        res = jnp.dot(
            turned[...], weights[k, :, pl.ds(at, 256)], preferred_element_type=F32
        ).astype(BF)
        for t in range(pairs):
            staged[k, t, :, pl.ds(at, 256)] = res[t * 256 : (t + 1) * 256]

    for c in range(3):
        for k in range(2):
            fetch(k, c).wait()
        if c == 0:
            for k in range(2):
                fetch(k, 2).start()
        for k in range(2):
            for at in (0, 256):
                tile(k, CHUNKS[c][0] + at)
        if c < 2:
            for k in range(2):
                put(k, c, 0).start()
                put(k, c, 1).start()

    last = pl.ds(1536, 128)
    both = jnp.concatenate((weights[0, :, last], weights[1, :, last]), axis=1)
    res = jnp.dot(turned[...], both, preferred_element_type=F32).astype(BF)
    for t in range(pairs):
        for k in range(2):
            staged[k, t, :, last] = res[t * 256 : (t + 1) * 256, k * 128 : (k + 1) * 128]
    for k in range(2):
        put(k, 2, 0).start()
        put(k, 2, 1).start()
    for c in range(3):
        for k in range(2):
            put(k, c, 0).wait()
            put(k, c, 1).wait()


def project(info, tokens, gate, up, after=()):
    sizes = [mine.shape[0] for mine, _ in tokens]
    tokens = [block for both in tokens for block in both]
    pairs = sum(sizes)
    columns = 1664
    whole = pl.BlockSpec(memory_space=pltpu.VMEM)
    far = pl.BlockSpec(memory_space=pltpu.HBM)
    shape = jax.ShapeDtypeStruct((2, pairs, 128, columns), BF)
    return pl.pallas_call(
        functools.partial(project_body, sizes),
        in_specs=[pl.BlockSpec(memory_space=pltpu.SMEM)]
        + [whole] * len(tokens)
        + [far] * 2
        + [pl.BlockSpec(memory_space=pl.ANY)] * len(after),
        out_specs=[pl.BlockSpec(memory_space=pl.ANY)] * 2,
        scratch_shapes=[
            pltpu.VMEM((256 * pairs, 1024), BF),
            pltpu.VMEM((256 * pairs, 1024), BF),
            pltpu.VMEM((2, 1024, columns), BF),
            pltpu.VMEM((2, pairs, 256, columns), BF),
            pltpu.SemaphoreType.DMA((2, 3)),
            pltpu.SemaphoreType.DMA((2, 3, 2)),
        ],
        out_shape=[shape] * 2,
        compiler_params=pltpu.CompilerParams(vmem_limit_bytes=24 << 20),
        cost_estimate=pl.CostEstimate(flops=COST, bytes_accessed=COST, transcendentals=0),
        name="project",
    )(info, *tokens, gate, up, *after)


def down_body(first, last, depth, info, *refs):
    rows, weight = refs[:2]
    weights, sem = refs[-2:]
    outs = refs[-4:-2] if last else refs[-3:-2]
    start = pl.multiple_of(info[1], 128)

    def fetch(j):
        columns = pl.ds(j * 256, 256)
        source = weight.at[pl.ds(start, depth), columns]
        return pltpu.make_async_copy(source, weights.at[:, columns], sem.at[j])

    for j in range(4):
        fetch(j).start()
    left = jnp.concatenate((rows[0], rows[1]), axis=0)
    for j in range(4):
        fetch(j).wait()
        columns = pl.ds(j * 256, 256)
        res = jnp.dot(left, weights[:, columns], preferred_element_type=F32)
        if first:
            outs[0][:, columns] = res
            continue
        for t in range(2):
            for r in range(16):
                place = r ^ info[0]
                if r < 8:
                    value = res[t * 128 + r * 16 : t * 128 + (r + 1) * 16]
                else:
                    value = refs[2][pl.ds(t * 128 + (r - 8) * 16, 16), columns]
                if not last:
                    outs[0][t, pl.ds(pl.multiple_of(place * 16, 16), 16), columns] = value
                    continue
                value = value + refs[3][t, pl.ds(pl.multiple_of(place * 16, 16), 16), columns]
                spot = pl.ds(pl.multiple_of((place & 7) * 16, 16), 16)

                @pl.when(place < 8)
                def _():
                    outs[1][t, spot, columns] = value

                @pl.when(place >= 8)
                def _():
                    outs[0][t, spot, columns] = value.astype(BF)


def down(info, rows, weight, half=None, before=None, after=()):
    depth = rows.shape[2]
    first, last = half is None, before is not None
    extra = [a for a in (half, before) if a is not None]
    if first:
        shapes = [jax.ShapeDtypeStruct((256, 1024), F32)]
    elif last:
        shapes = [
            jax.ShapeDtypeStruct((2, 128, 1024), BF),
            jax.ShapeDtypeStruct((2, 128, 1024), F32),
        ]
    else:
        shapes = [jax.ShapeDtypeStruct((2, 256, 1024), F32)]
    whole = pl.BlockSpec(memory_space=pltpu.VMEM)
    anywhere = pl.BlockSpec(memory_space=pl.ANY)
    out = pl.pallas_call(
        functools.partial(down_body, first, last, depth),
        in_specs=[pl.BlockSpec(memory_space=pltpu.SMEM), whole, anywhere]
        + [whole] * len(extra)
        + [anywhere] * len(after),
        out_specs=[whole] * len(shapes),
        out_shape=shapes,
        scratch_shapes=[pltpu.VMEM((depth, 1024), BF), pltpu.SemaphoreType.DMA((4,))],
        compiler_params=pltpu.CompilerParams(vmem_limit_bytes=24 << 20),
        cost_estimate=pl.CostEstimate(flops=COST, bytes_accessed=COST, transcendentals=0),
        name="down",
    )(info, rows, weight, *extra, *after)
    return out if last else out[0]


def halves_body(count, before, *refs):
    keeps, cames = refs[:count], refs[count : 2 * count]
    send, keep = refs[-2:]
    half = keep.shape[2]
    at = 0
    if before:
        old_send, old_keep = refs[2 * count : 2 * count + 2]
        at = old_send.shape[1]
        send[:, :at] = old_send[...]
        keep[:, :at] = old_keep[...]
    for old, came in zip(keeps, cames):
        spans = old.shape[1]
        for k in range(2):
            for t in range(spans):
                total = old[k, t].astype(F32) + came[k, t].astype(F32)
                send[k, at + t] = total[:half].astype(BF)
                keep[k, at + t] = total[half:].astype(BF)
        at += spans


def hidden_body(keep, came, *refs):
    gate = keep[0].astype(F32) + came[0].astype(F32)
    up = keep[1].astype(F32) + came[1].astype(F32)
    refs[-1][...] = (gate / (1.0 + jnp.exp(-gate)) * up).astype(BF)


def stack_body(first, second, *refs):
    refs[-1][0] = first[...]
    refs[-1][1] = second[...]


def join_body(theirs, mine, *refs):
    rows = mine.shape[1]
    refs[-1][:, :rows] = theirs[...]
    refs[-1][:, rows:] = mine[...]


def call(body, name, args, shapes, after):
    return pl.pallas_call(
        body,
        in_specs=[pl.BlockSpec(memory_space=pltpu.VMEM)] * len(args)
        + [pl.BlockSpec(memory_space=pl.ANY)] * len(after),
        out_specs=[pl.BlockSpec(memory_space=pltpu.VMEM)] * len(shapes),
        out_shape=[jax.ShapeDtypeStruct(shape, BF) for shape in shapes],
        compiler_params=pltpu.CompilerParams(vmem_limit_bytes=16 << 20),
        cost_estimate=pl.CostEstimate(flops=COST, bytes_accessed=COST, transcendentals=0),
        name=name,
    )(*args, *after)


def halves(keeps, cames, done=(), after=()):
    spans = sum(part.shape[1] for part in (*keeps, *done[:1]))
    _, _, rows, columns = keeps[0].shape
    shape = (2, spans, rows // 2, columns)
    body = functools.partial(halves_body, len(keeps), bool(done))
    return call(body, "halves", (*keeps, *cames, *done), [shape] * 2, after)


def hidden(keep, came, after):
    return call(hidden_body, "hidden", (keep, came), [keep.shape[1:]], after)[0]


def join(theirs, mine, after):
    spans, rows, columns = mine.shape
    return call(join_body, "join", (theirs, mine), [(spans, 2 * rows, columns)], after)[0]


def cut_body(axis, count, info, *refs):
    sources, targets, sem = refs[:count], refs[-count - 1 : -1], refs[-1]
    copies = []
    for i in range(count):
        size = targets[i].shape[axis]
        part = pl.ds(pl.multiple_of(info[0], 128), size)
        source = sources[i].at[part] if axis == 0 else sources[i].at[:, part]
        copies.append(pltpu.make_async_copy(source, targets[i], sem.at[i]))
    for copy in copies:
        copy.start()
    for copy in copies:
        copy.wait()


def cut(start, size, axis, weights, after):
    count = len(weights)
    shapes = []
    for weight in weights:
        shape = list(weight.shape)
        shape[axis] = size
        shapes.append(jax.ShapeDtypeStruct(tuple(shape), BF))
    anywhere = pl.BlockSpec(memory_space=pl.ANY)
    return pl.pallas_call(
        functools.partial(cut_body, axis, count),
        in_specs=[pl.BlockSpec(memory_space=pltpu.SMEM)] + [anywhere] * (count + len(after)),
        out_specs=[anywhere] * count,
        out_shape=shapes,
        scratch_shapes=[pltpu.SemaphoreType.DMA((count,))],
        compiler_params=pltpu.CompilerParams(vmem_limit_bytes=16 << 20),
        cost_estimate=pl.CostEstimate(flops=COST, bytes_accessed=COST, transcendentals=0),
        name="cut",
    )(jnp.reshape(start, (1,)), *weights, *after)


def stack(first, second, after):
    return call(stack_body, "stack", (first, second), [(2, *first.shape)], after)[0]


class Line:
    def __init__(self):
        self.last = ()

    def __call__(self, kernel, *args, also=()):
        out = kernel(*args, after=(*self.last, *also))
        self.last = (out[0] if isinstance(out, (list, tuple)) else out,)
        return out


TURNS = "0jg1u00203w12030120312012310231032103122301323"


def local(tokens, gate_weight, up_weight, down_weight):
    core = lax.axis_index("group") % 2
    masks = jnp.asarray(mask_table())[core, :, lax.axis_index("mp")]
    columns = gate_weight.shape[1] // 2
    line = Line()

    def info(flow, offset):
        return jnp.stack((masks[flow], jnp.asarray(offset, jnp.int32)))

    def fetch(shift):
        return lax.ppermute(tokens, "group", group_pairs(-shift))

    after, before, opposite = fetch(1), fetch(-1), fetch(2)
    far = opposite[None]
    near = pltpu.with_memory_space_constraint(tokens[None], pltpu.HBM)
    group_near = (near, swap(tokens)[None])
    group_far = (far, swap(far))

    mine = core * columns
    given = (1 - core) * columns
    own_weights = [
        pltpu.with_memory_space_constraint(w, pltpu.HBM) for w in (gate_weight, up_weight)
    ]
    own_down = pltpu.with_memory_space_constraint(down_weight, pltpu.HBM)
    got = {}

    def unit(u, groups, weights, offset):
        flow = u % 2
        done = ()
        for i, group in enumerate(groups):
            send, keep = line(
                project, info(flow, offset), [got[name] for name in group], *(got[w] for w in weights)
            )
            came = exchange(send, flow, 0)
            yield None
            done = line(halves, [keep], [came], done)
            yield None
        send, keep = done
        for step in (1, 2):
            send, keep = line(halves, [keep], [exchange(send, flow, step)])
            yield None
        rows = line(hidden, keep, exchange(send, flow, 3))
        yield None
        for step in (3, 2, 1):
            rows = line(join, exchange(rows, flow, step), rows)
            yield None
        theirs = exchange(rows, flow, 0)
        weight, place = got["down" if u < 2 else "down_other"]
        half = line(down, info(flow, place), rows, weight)
        yield None
        before = got[u - 2] if u >= 2 else None
        got[u] = line(down, info(flow, place), theirs, weight, half, before)
        yield None

    got["near"], got["far"] = group_near, group_far
    got["gate"], got["up"] = own_weights
    units = (
        unit(0, (("near",), ("far",)), ("gate", "up"), mine),
        unit(1, (("sides",),), ("gate", "up"), mine),
        unit(2, (("near", "far"),), ("gate_other", "up_other"), 0),
        unit(3, (("sides",),), ("gate_other", "up_other"), 0),
    )
    got["down"] = own_down, mine
    for turn in TURNS:
        if turn in "gu":
            name = "gate" if turn == "g" else "up"
            got[name + "_other"] = swap(line(cut, given, columns, 1, [got[name]])[0])
            continue
        if turn == "w":
            got["down_other"] = swap(line(cut, given, columns, 0, [own_down])[0]), 0
            continue
        if turn == "j":
            sides = line(stack, after, before, also=(opposite,))
            got["sides"] = (sides, swap(sides))
            continue
        next(units[int(turn)])
    (a_send, a_keep), (b_send, b_keep) = got[2], got[3]

    a_total = a_keep + swap(a_send).astype(F32)
    b_total = b_keep + swap(b_send).astype(F32)
    from_opposite = lax.ppermute(a_total[1].astype(BF), "group", group_pairs(2))
    from_before = lax.ppermute(b_total[0].astype(BF), "group", group_pairs(1))
    from_after = lax.ppermute(b_total[1].astype(BF), "group", group_pairs(-1))
    total = a_total[0] + from_opposite.astype(F32)
    total = total + from_before.astype(F32) + from_after.astype(F32)
    return total.astype(BF)


def solution(mesh):
    placed = (P("group", "mp"), P("mp", "group"), P("mp", "group"), P("group", "mp"))
    return jax.shard_map(
        local, mesh=mesh, in_specs=placed, out_specs=P("group", "mp"), check_vma=False
    )
```

```python
import functools

import jax
import jax.numpy as jnp
from jax import lax
from jax.experimental import pallas as pl
from jax.experimental.pallas import tpu as pltpu
from jax.sharding import PartitionSpec as P

BF = jnp.bfloat16
F32 = jnp.float32

TIMES = {
    "project": 5.0,
    "cut": 3.0,
    "down": 2.5,
    "halves": 2.0,
    "hidden": 2.0,
    "join": 2.0,
    "stack": 1.0,
}

PAIR = {"e": (1, 0, 3, 2), "o": (3, 2, 1, 0)}
ORDERS = (
    (("x", "e"), ("x", "o"), ("y", "e"), ("y", "o")),
    (("x", "o"), ("x", "e"), ("y", "o"), ("y", "e")),
), (
    (("y", "e"), ("y", "o"), ("x", "e"), ("x", "o")),
    (("y", "o"), ("y", "e"), ("x", "o"), ("x", "e")),
)
SWAP = [(g, g ^ 1) for g in range(8)]

HALF = 1664
WIDE = (896, 768)
DOWN = (512, 512)

VMEM = pl.BlockSpec(memory_space=pltpu.VMEM)
ANY = pl.BlockSpec(memory_space=pl.ANY)


def partner(m, link):
    axis, kind = link
    x, y = divmod(m, 4)
    return 4 * PAIR[kind][x] + y if axis == "x" else 4 * x + PAIR[kind][y]


def exchange(a, flow, step):
    pairs = [
        (g * 16 + m, g * 16 + partner(m, ORDERS[g % 2][flow][step]))
        for g in range(8)
        for m in range(16)
    ]
    return lax.ppermute(a, ("group", "mp"), pairs)


def swap(a):
    return lax.ppermute(a, "group", SWAP)


def shift(a, chips):
    return lax.ppermute(a, "group", [(g, (g + 2 * chips) % 8) for g in range(8)])


def core_index():
    return lax.axis_index("group") & 1


def mask_of(flow):
    place = lax.axis_index("mp")
    x, y = place >> 2, place & 3
    lead = x + core_index() * (y - x)
    rest = x + y - lead
    own = 0
    for at in (lead, rest):
        even, odd = ((at + 1) >> 1) & 1, at >> 1
        own = own * 4 + (2 * even + odd if flow == 0 else 2 * odd + even)
    return 15 ^ own


def kernel(body, name, args, shapes, after, scratch=(), limit=2, specs=None):
    specs = specs or [VMEM] * len(args)
    return pl.pallas_call(
        body,
        in_specs=specs + [ANY] * len(after),
        out_specs=[VMEM] * len(shapes),
        out_shape=shapes,
        scratch_shapes=list(scratch),
        compiler_params=pltpu.CompilerParams(vmem_limit_bytes=limit << 20),
        cost_estimate=pl.CostEstimate(
            flops=int(TIMES[name] * 1.15e9), bytes_accessed=0, transcendentals=0
        ),
        name=name,
    )(*args, *after)


def cut_body(axis, pieces, source, *refs):
    outs, sem = refs[-1 - 2 * len(pieces) : -1], refs[-1]
    copies = []
    for which in range(2):
        core = core_index()
        begin = (core if which else 1 - core) * HALF
        at = 0
        for i, size in enumerate(pieces):
            if axis == 1:
                place = source.at[:, pl.ds(pl.multiple_of(begin + at, 128), size)]
            else:
                place = source.at[pl.ds(pl.multiple_of(begin, 128), HALF), pl.ds(at, size)]
            at += size
            n = which * len(pieces) + i
            copies.append(pltpu.make_async_copy(place, outs[n], sem.at[n]))
    for copy in copies:
        copy.start()
    for copy in copies:
        copy.wait()


def cut(axis, pieces, weight, after=()):
    weight = pltpu.with_memory_space_constraint(weight, pltpu.HBM)
    rows = weight.shape[0] if axis == 1 else HALF
    shapes = [pltpu.VMEM((rows, size), BF) for size in pieces] * 2
    out = kernel(
        functools.partial(cut_body, axis, pieces),
        "cut",
        (weight,),
        shapes,
        after,
        [pltpu.SemaphoreType.DMA((2 * len(pieces),))],
        specs=[pl.BlockSpec(memory_space=pltpu.HBM)],
    )
    return out[: len(pieces)], out[len(pieces) :]


def project_body(flow, sizes, *refs):
    count = 2 * len(sizes)
    blocks = refs[:count]
    weights = (refs[count : count + 2], refs[count + 2 : count + 4])
    send, keep, plain, turned = refs[-4:]
    pairs = sum(sizes)
    mask = mask_of(flow)
    at = 0
    for i, size in enumerate(sizes):
        for t in range(size):
            plain[pl.ds(at, 128)] = blocks[2 * i][t]
            plain[pl.ds(at + 128, 128)] = blocks[2 * i + 1][t]
            at += 256
    for t in range(pairs):
        for r in range(16):
            source = pl.multiple_of(t * 256 + (r ^ mask) * 16, 16)
            turned[pl.ds(t * 256 + r * 16, 16)] = plain[pl.ds(source, 16)]

    def store(k, columns, part):
        for t in range(pairs):
            send[k, t, :, columns] = part[t * 256 : t * 256 + 128]
            keep[k, t, :, columns] = part[t * 256 + 128 : t * 256 + 256]

    def multiply(weight):
        return jnp.dot(turned[...], weight, preferred_element_type=F32).astype(BF)

    for piece, base in ((0, 0), (1, WIDE[0])):
        for k in range(2):
            for at in range(0, 768, 256):
                part = multiply(weights[k][piece][:, at : at + 256])
                store(k, pl.ds(base + at, 256), part)
    both = jnp.concatenate((weights[0][0][:, 768:], weights[1][0][:, 768:]), axis=1)
    res = multiply(both)
    for k in range(2):
        store(k, pl.ds(768, 128), res[:, k * 128 : (k + 1) * 128])


def project(flow, tokens, gate, up, after=()):
    sizes = [mine.shape[0] for mine, _ in tokens]
    blocks = [block for both in tokens for block in both]
    rows = 256 * sum(sizes)
    shape = jax.ShapeDtypeStruct((2, sum(sizes), 128, HALF), BF)
    return kernel(
        functools.partial(project_body, flow, sizes),
        "project",
        (*blocks, *gate, *up),
        [shape] * 2,
        after,
        [pltpu.VMEM((rows, 1024), BF)] * 2,
        8,
    )


def down_body(flow, first, last, *refs):
    rows, pieces, refs = refs[0], refs[1:3], refs[3:]
    outs = refs[-1:]
    mask = mask_of(flow)
    left = jnp.concatenate((rows[0], rows[1]), axis=0)
    for j in range(4):
        columns = pl.ds(j * 256, 256)
        weight = pieces[j // 2][:, j % 2 * 256 : (j % 2 + 1) * 256]
        res = jnp.dot(left, weight, preferred_element_type=F32)
        if first:
            outs[0][:, columns] = res
            continue
        for t in range(2):
            for r in range(16):
                place = r ^ mask
                if r < 8:
                    value = res[t * 128 + r * 16 : t * 128 + (r + 1) * 16]
                else:
                    value = refs[0][pl.ds(t * 128 + (r - 8) * 16, 16), columns]
                spot = pl.ds(pl.multiple_of(place * 16, 16), 16)
                outs[0][t, spot, columns] = value
    if last:
        send, keep, total = refs[-3:]
        keep[...] = total[:, :128] + refs[1][:, :128]
        send[...] = (total[:, 128:] + refs[1][:, 128:]).astype(BF)


def down(flow, rows, weights, half=None, before=None, after=()):
    first, last = half is None, before is not None
    if first:
        shapes = [jax.ShapeDtypeStruct((256, 1024), F32)]
    elif last:
        shapes = [
            jax.ShapeDtypeStruct((2, 128, 1024), BF),
            jax.ShapeDtypeStruct((2, 128, 1024), F32),
        ]
    else:
        shapes = [jax.ShapeDtypeStruct((2, 256, 1024), F32)]
    extra = [a for a in (half, before) if a is not None]
    out = kernel(
        functools.partial(down_body, flow, first, last),
        "down",
        (rows, *weights, *extra),
        shapes,
        after,
        [pltpu.VMEM((2, 256, 1024), F32)] if last else (),
        limit=4,
    )
    return out if last else out[0]


def halves_body(keep, came, *refs):
    send, kept = refs[-2:]
    half = kept.shape[2]
    for k in range(2):
        for t in range(2):
            total = keep[k, t].astype(F32) + came[k, t].astype(F32)
            send[k, t] = total[:half].astype(BF)
            kept[k, t] = total[half:].astype(BF)


def halves(keep, came, after):
    shape = jax.ShapeDtypeStruct((2, 2, keep.shape[2] // 2, HALF), BF)
    return kernel(halves_body, "halves", (keep, came), [shape] * 2, after)


def hidden_body(keep, came, *refs):
    gate = keep[0].astype(F32) + came[0].astype(F32)
    up = keep[1].astype(F32) + came[1].astype(F32)
    refs[-1][...] = (gate / (1.0 + jnp.exp(-gate)) * up).astype(BF)


def hidden(keep, came, after):
    shape = jax.ShapeDtypeStruct(keep.shape[1:], BF)
    return kernel(hidden_body, "hidden", (keep, came), [shape], after)[0]


def join_body(theirs, mine, *refs):
    rows = mine.shape[1]
    refs[-1][:, :rows] = theirs[...]
    refs[-1][:, rows:] = mine[...]


def join(theirs, mine, after):
    shape = jax.ShapeDtypeStruct((2, 2 * mine.shape[1], HALF), BF)
    return kernel(join_body, "join", (theirs, mine), [shape], after)[0]


def stack_body(first, second, *refs):
    refs[-1][0] = first[...]
    refs[-1][1] = second[...]


def stack(first, second, after):
    shape = jax.ShapeDtypeStruct((2, *first.shape), BF)
    return kernel(stack_body, "stack", (first, second), [shape], after)[0]


class Line:
    def __init__(self):
        self.last = ()

    def __call__(self, call, *args):
        out = call(*args, after=self.last)
        first = out
        while isinstance(first, (list, tuple)):
            first = first[0]
        self.last = (first,)
        return out


TURNS = "guj0123013120130123123103210230w230221301302"


def local(tokens, gate_weight, up_weight, down_weight):
    line = Line()
    after, before = shift(tokens, -1), shift(tokens, 1)
    near, beside = tokens[None], swap(tokens)[None]
    far = shift(beside, 2)
    pair_a = [(near, beside), (swap(far), far)]
    weights = {"g": (1, WIDE, gate_weight), "u": (1, WIDE, up_weight), "w": (0, DOWN, down_weight)}
    own, other = {}, {}
    sides = []
    finished = {}

    def unit(u):
        flow = u % 2
        held = own if u < 2 else other
        send, keep = line(project, flow, pair_a if flow == 0 else sides, held["g"], held["u"])
        for step in range(3):
            came = exchange(send, flow, step)
            yield
            send, keep = line(halves, keep, came)
        came = exchange(send, flow, 3)
        yield
        rows = line(hidden, keep, came)
        for step in (3, 2, 1):
            theirs = exchange(rows, flow, step)
            yield
            rows = line(join, theirs, rows)
        theirs = exchange(rows, flow, 0)
        yield
        half = line(down, flow, rows, held["w"])
        yield
        finished[u] = line(down, flow, theirs, held["w"], half, finished.get(u - 2))
        yield

    units = [unit(u) for u in range(4)]
    for turn in TURNS:
        if turn in weights:
            given, own[turn] = line(cut, *weights[turn])
            other[turn] = [swap(piece) for piece in given]
        elif turn == "j":
            both = line(stack, after, before)
            sides.append((both, swap(both)))
        else:
            next(units[int(turn)])

    (a_send, a_keep), (b_send, b_keep) = finished[2], finished[3]
    a_total = a_keep + swap(a_send).astype(F32)
    b_total = b_keep + swap(b_send).astype(F32)
    from_opposite = shift(a_total[1].astype(BF), 2)
    from_before = shift(b_total[0].astype(BF), 1)
    from_after = shift(b_total[1].astype(BF), -1)
    total = a_total[0] + from_opposite.astype(F32)
    total = total + from_before.astype(F32) + from_after.astype(F32)
    return total.astype(BF)


def solution(mesh):
    placed = (P("group", "mp"), P("mp", "group"), P("mp", "group"), P("group", "mp"))
    return jax.shard_map(
        local, mesh=mesh, in_specs=placed, out_specs=P("group", "mp"), check_vma=False
    )
```

```python
import functools

import jax
import jax.numpy as jnp
from jax import lax
from jax.experimental import pallas as pl
from jax.experimental.pallas import tpu as pltpu
from jax.sharding import PartitionSpec as P

BF = jnp.bfloat16
F32 = jnp.float32

TIMES = {
    "down": 2.5,
    "halves": 2.0,
    "hidden": 2.0,
    "join": 2.0,
    "stack": 1.0,
}

PAIR = {"e": (1, 0, 3, 2), "o": (3, 2, 1, 0)}
ORDERS = (
    (("x", "e"), ("x", "o"), ("y", "e"), ("y", "o")),
    (("x", "o"), ("x", "e"), ("y", "o"), ("y", "e")),
), (
    (("y", "e"), ("y", "o"), ("x", "e"), ("x", "o")),
    (("y", "o"), ("y", "e"), ("x", "o"), ("x", "e")),
)
SWAP = [(g, g ^ 1) for g in range(8)]

HALF = 1664
WIDE = (896, 768)
DOWN = (512, 512)

VMEM = pl.BlockSpec(memory_space=pltpu.VMEM)
ANY = pl.BlockSpec(memory_space=pl.ANY)


def partner(m, link):
    axis, kind = link
    x, y = divmod(m, 4)
    return 4 * PAIR[kind][x] + y if axis == "x" else 4 * x + PAIR[kind][y]


def exchange(a, flow, step):
    pairs = [
        (g * 16 + m, g * 16 + partner(m, ORDERS[g % 2][flow][step]))
        for g in range(8)
        for m in range(16)
    ]
    return lax.ppermute(a, ("group", "mp"), pairs)


def swap(a):
    return lax.ppermute(a, "group", SWAP)


def shift(a, chips):
    return lax.ppermute(a, "group", [(g, (g + 2 * chips) % 8) for g in range(8)])


def core_index():
    return lax.axis_index("group") & 1


def mask_of(flow):
    place = lax.axis_index("mp")
    x, y = place >> 2, place & 3
    lead = x + core_index() * (y - x)
    rest = x + y - lead
    own = 0
    for at in (lead, rest):
        even, odd = ((at + 1) >> 1) & 1, at >> 1
        own = own * 4 + (2 * even + odd if flow == 0 else 2 * odd + even)
    return 15 ^ own


def kernel(body, name, args, shapes, after, scratch=(), limit=2, specs=None, time=None):
    specs = specs or [VMEM] * len(args)
    return pl.pallas_call(
        body,
        in_specs=specs + [ANY] * len(after),
        out_specs=[VMEM] * len(shapes),
        out_shape=shapes,
        scratch_shapes=list(scratch),
        compiler_params=pltpu.CompilerParams(vmem_limit_bytes=limit << 20),
        cost_estimate=pl.CostEstimate(
            flops=int((time or TIMES[name]) * 1.15e9), bytes_accessed=0, transcendentals=0
        ),
        name=name,
    )(*args, *after)


def cut_body(axis, pieces, parts, count, *refs):
    sources, outs, sem = refs[:count], refs[-1 - count * len(parts) * len(pieces) : -1], refs[-1]
    copies = []
    core = core_index()
    for source in sources:
        for part in parts:
            begin = (core if part == "own" else 1 - core) * HALF
            at = 0
            for size in pieces:
                if axis == 1:
                    place = source.at[:, pl.ds(pl.multiple_of(begin + at, 128), size)]
                else:
                    place = source.at[pl.ds(pl.multiple_of(begin, 128), HALF), pl.ds(at, size)]
                at += size
                n = len(copies)
                copies.append(pltpu.make_async_copy(place, outs[n], sem.at[n]))
    for copy in copies:
        copy.start()
    for copy in copies:
        copy.wait()


def cut(axis, pieces, parts, weights, after=()):
    weights = [pltpu.with_memory_space_constraint(w, pltpu.HBM) for w in weights]
    rows = weights[0].shape[0] if axis == 1 else HALF
    shapes = [pltpu.VMEM((rows, size), BF) for size in pieces] * (len(parts) * len(weights))
    out = kernel(
        functools.partial(cut_body, axis, pieces, parts, len(weights)),
        "cut",
        weights,
        shapes,
        after,
        [pltpu.SemaphoreType.DMA((len(shapes),))],
        specs=[pl.BlockSpec(memory_space=pltpu.HBM)] * len(weights),
        time=1.5 * len(weights) * len(parts),
    )
    return [out[i : i + len(pieces)] for i in range(0, len(out), len(pieces))]


def hold_body(source, *refs):
    out, sem = refs[-2:]
    copy = pltpu.make_async_copy(source, out, sem)
    copy.start()
    copy.wait()


def hold(tokens, after):
    return kernel(
        hold_body,
        "stack",
        (pltpu.with_memory_space_constraint(tokens, pltpu.HBM),),
        [pltpu.VMEM(tokens.shape, BF)],
        after,
        [pltpu.SemaphoreType.DMA],
        specs=[pl.BlockSpec(memory_space=pltpu.HBM)],
    )[0]


def project_body(flow, sizes, *refs):
    count = 2 * len(sizes)
    blocks = refs[:count]
    weights = (refs[count : count + 2], refs[count + 2 : count + 4])
    send, keep, plain, turned = refs[-4:]
    pairs = sum(sizes)
    mask = mask_of(flow)
    at = 0
    for i, size in enumerate(sizes):
        for t in range(size):
            plain[pl.ds(at, 128)] = blocks[2 * i][t]
            plain[pl.ds(at + 128, 128)] = blocks[2 * i + 1][t]
            at += 256
    for t in range(pairs):
        for r in range(16):
            source = pl.multiple_of(t * 256 + (r ^ mask) * 16, 16)
            turned[pl.ds(t * 256 + r * 16, 16)] = plain[pl.ds(source, 16)]

    def store(k, columns, part):
        for t in range(pairs):
            send[k, t, :, columns] = part[t * 256 : t * 256 + 128]
            keep[k, t, :, columns] = part[t * 256 + 128 : t * 256 + 256]

    def multiply(weight):
        return jnp.dot(turned[...], weight, preferred_element_type=F32).astype(BF)

    for piece, base in ((0, 0), (1, WIDE[0])):
        for k in range(2):
            for at in range(0, 768, 256):
                part = multiply(weights[k][piece][:, at : at + 256])
                store(k, pl.ds(base + at, 256), part)
    both = jnp.concatenate((weights[0][0][:, 768:], weights[1][0][:, 768:]), axis=1)
    res = multiply(both)
    for k in range(2):
        store(k, pl.ds(768, 128), res[:, k * 128 : (k + 1) * 128])


def project(flow, tokens, gate, up, after=()):
    sizes = [mine.shape[0] for mine, _ in tokens]
    blocks = [block for both in tokens for block in both]
    rows = 256 * sum(sizes)
    shape = jax.ShapeDtypeStruct((2, sum(sizes), 128, HALF), BF)
    return kernel(
        functools.partial(project_body, flow, sizes),
        "project",
        (*blocks, *gate, *up),
        [shape] * 2,
        after,
        [pltpu.VMEM((rows, 1024), BF)] * 2,
        8,
        time=1.5,
    )


def down_body(flow, first, last, *refs):
    rows, pieces, refs = refs[0], refs[1:3], refs[3:]
    outs = refs[-1:]
    mask = mask_of(flow)
    left = jnp.concatenate((rows[0], rows[1]), axis=0)
    for j in range(4):
        columns = pl.ds(j * 256, 256)
        weight = pieces[j // 2][:, j % 2 * 256 : (j % 2 + 1) * 256]
        res = jnp.dot(left, weight, preferred_element_type=F32)
        if first:
            outs[0][:, columns] = res
            continue
        for t in range(2):
            for r in range(16):
                place = r ^ mask
                if r < 8:
                    value = res[t * 128 + r * 16 : t * 128 + (r + 1) * 16]
                else:
                    value = refs[0][pl.ds(t * 128 + (r - 8) * 16, 16), columns]
                spot = pl.ds(pl.multiple_of(place * 16, 16), 16)
                outs[0][t, spot, columns] = value
    if last:
        send, keep, total = refs[-3:]
        keep[...] = total[:, :128] + refs[1][:, :128]
        send[...] = (total[:, 128:] + refs[1][:, 128:]).astype(BF)


def down(flow, rows, weights, half=None, before=None, after=()):
    first, last = half is None, before is not None
    if first:
        shapes = [jax.ShapeDtypeStruct((256, 1024), F32)]
    elif last:
        shapes = [
            jax.ShapeDtypeStruct((2, 128, 1024), BF),
            jax.ShapeDtypeStruct((2, 128, 1024), F32),
        ]
    else:
        shapes = [jax.ShapeDtypeStruct((2, 256, 1024), F32)]
    extra = [a for a in (half, before) if a is not None]
    out = kernel(
        functools.partial(down_body, flow, first, last),
        "down",
        (rows, *weights, *extra),
        shapes,
        after,
        [pltpu.VMEM((2, 256, 1024), F32)] if last else (),
        limit=4,
    )
    return out if last else out[0]


def halves_body(before, keep, came, *refs):
    send, kept = refs[-2:]
    half = kept.shape[2]
    at = 0
    if before:
        old_send, old_kept = refs[:2]
        at = old_send.shape[1]
        send[:, :at] = old_send[...]
        kept[:, :at] = old_kept[...]
    for k in range(2):
        for t in range(keep.shape[1]):
            total = keep[k, t].astype(F32) + came[k, t].astype(F32)
            send[k, at + t] = total[:half].astype(BF)
            kept[k, at + t] = total[half:].astype(BF)


def halves(keep, came, done=(), after=()):
    spans = keep.shape[1] + (done[0].shape[1] if done else 0)
    shape = jax.ShapeDtypeStruct((2, spans, keep.shape[2] // 2, HALF), BF)
    body = functools.partial(halves_body, bool(done))
    return kernel(body, "halves", (keep, came, *done), [shape] * 2, after)


def add_body(keep, came, *refs):
    refs[-1][...] = (keep[...].astype(F32) + came[...].astype(F32)).astype(BF)


def add(keep, came, after):
    return kernel(add_body, "halves", (keep, came), [jax.ShapeDtypeStruct(keep.shape, BF)], after)[0]


def hidden_body(mine, theirs, *refs):
    half = mine.shape[2] // 2
    for at, other in ((0, half), (half, 0)):
        gate = mine[0, :, at : at + half].astype(F32) + theirs[0, :, other : other + half].astype(F32)
        up = mine[1, :, at : at + half].astype(F32) + theirs[1, :, other : other + half].astype(F32)
        refs[-1][:, at : at + half] = (gate / (1.0 + jnp.exp(-gate)) * up).astype(BF)


def hidden(mine, theirs, after):
    shape = jax.ShapeDtypeStruct(mine.shape[1:], BF)
    return kernel(hidden_body, "hidden", (mine, theirs), [shape], after)[0]


def join_body(theirs, mine, *refs):
    rows = mine.shape[1]
    refs[-1][:, :rows] = theirs[...]
    refs[-1][:, rows:] = mine[...]


def join(theirs, mine, after):
    shape = jax.ShapeDtypeStruct((2, 2 * mine.shape[1], HALF), BF)
    return kernel(join_body, "join", (theirs, mine), [shape], after)[0]


def stack_body(first, second, *refs):
    refs[-1][0] = first[...]
    refs[-1][1] = second[...]


def stack(first, second, after):
    shape = jax.ShapeDtypeStruct((2, *first.shape), BF)
    return kernel(stack_body, "stack", (first, second), [shape], after)[0]


class Line:
    def __init__(self):
        self.last = ()

    def __call__(self, call, *args):
        out = call(*args, after=self.last)
        first = out
        while isinstance(first, (list, tuple)):
            first = first[0]
        self.last = (first,)
        return out


TURNS = "oguj012301w230123012301230123012301230213"


def local(tokens, gate_weight, up_weight, down_weight):
    line = Line()
    after, before = shift(tokens, -1), shift(tokens, 1)
    beside, far = swap(tokens), shift(tokens, 2)
    near = line(hold, tokens)
    pair_a = [(near[None], beside[None]), (far[None], swap(far)[None])]
    sides = []
    own, other = {}, {}
    finished = {}

    def unit(u):
        flow = u % 2
        held = own if u < 2 else other
        groups = [sides] if flow else [pair_a]
        parts = []
        for group in groups:
            send, keep = line(project, flow, group, held["g"], held["u"])
            parts.append((keep, exchange(send, flow, 0)))
            yield
        done = ()
        for i, part in enumerate(parts):
            if i:
                yield
            done = line(halves, *part, done)
        send, keep = done
        came = exchange(send, flow, 1)
        yield
        send, keep = line(halves, keep, came)
        came = exchange(send, flow, 2)
        yield
        rows = line(add, keep, came)
        came = exchange(rows, flow, 3)
        yield
        rows = line(hidden, rows, came)
        for step in (2, 1):
            theirs = exchange(rows, flow, step)
            yield
            rows = line(join, theirs, rows)
        theirs = exchange(rows, flow, 0)
        yield
        half = line(down, flow, rows, held["w"])
        yield
        finished[u] = line(down, flow, theirs, held["w"], half, finished.get(u - 2))
        yield

    units = [unit(u) for u in range(4)]
    for turn in TURNS:
        if turn == "o":
            own["g"], own["u"] = line(cut, 1, WIDE, ("own",), (gate_weight, up_weight))
        elif turn in "gu":
            weight = gate_weight if turn == "g" else up_weight
            (given,) = line(cut, 1, WIDE, ("other",), (weight,))
            other[turn] = [swap(piece) for piece in given]
        elif turn == "w":
            own["w"], given = line(cut, 0, DOWN, ("own", "other"), (down_weight,))
            other["w"] = [swap(piece) for piece in given]
        elif turn == "j":
            both = line(stack, after, before)
            sides.append((both, swap(both)))
        else:
            next(units[int(turn)])

    (a_send, a_keep), (b_send, b_keep) = finished[2], finished[3]
    a_total = a_keep + swap(a_send).astype(F32)
    b_total = b_keep + swap(b_send).astype(F32)
    from_opposite = shift(a_total[1].astype(BF), 2)
    from_before = shift(b_total[0].astype(BF), 1)
    from_after = shift(b_total[1].astype(BF), -1)
    total = a_total[0] + from_opposite.astype(F32)
    total = total + from_before.astype(F32) + from_after.astype(F32)
    return total.astype(BF)


def solution(mesh):
    placed = (P("group", "mp"), P("mp", "group"), P("mp", "group"), P("group", "mp"))
    return jax.shard_map(
        local, mesh=mesh, in_specs=placed, out_specs=P("group", "mp"), check_vma=False
    )
```

```python
import functools

import jax
import jax.numpy as jnp
from jax import lax
from jax.experimental import pallas as pl
from jax.experimental.pallas import tpu as pltpu
from jax.sharding import PartitionSpec as P

BF = jnp.bfloat16
F32 = jnp.float32

TIMES = {
    "down": 0.4,
    "halves": 2.0,
    "hidden": 2.0,
    "join": 2.0,
    "stack": 0.1,
}

PAIR = {"e": (1, 0, 3, 2), "o": (3, 2, 1, 0)}
ORDERS = (
    (("x", "e"), ("x", "o"), ("y", "e"), ("y", "o")),
    (("x", "o"), ("x", "e"), ("y", "o"), ("y", "e")),
), (
    (("y", "e"), ("y", "o"), ("x", "e"), ("x", "o")),
    (("y", "o"), ("y", "e"), ("x", "o"), ("x", "e")),
)
SWAP = [(g, g ^ 1) for g in range(8)]

HALF = 1664
WIDE = (896, 768)
DOWN = (512, 512)

VMEM = pl.BlockSpec(memory_space=pltpu.VMEM)
ANY = pl.BlockSpec(memory_space=pl.ANY)


def partner(m, link):
    axis, kind = link
    x, y = divmod(m, 4)
    return 4 * PAIR[kind][x] + y if axis == "x" else 4 * x + PAIR[kind][y]


def exchange(a, flow, step):
    pairs = [
        (g * 16 + m, g * 16 + partner(m, ORDERS[g % 2][flow][step]))
        for g in range(8)
        for m in range(16)
    ]
    return lax.ppermute(a, ("group", "mp"), pairs)


def swap(a):
    return lax.ppermute(a, "group", SWAP)


def shift(a, chips):
    return lax.ppermute(a, "group", [(g, (g + 2 * chips) % 8) for g in range(8)])


def core_index():
    return lax.axis_index("group") & 1


def mask_of(flow):
    place = lax.axis_index("mp")
    x, y = place >> 2, place & 3
    lead = x + core_index() * (y - x)
    rest = x + y - lead
    own = 0
    for at in (lead, rest):
        even, odd = ((at + 1) >> 1) & 1, at >> 1
        own = own * 4 + (2 * even + odd if flow == 0 else 2 * odd + even)
    return 15 ^ own


def kernel(body, name, args, shapes, after, scratch=(), limit=2, specs=None, time=None):
    specs = specs or [VMEM] * len(args)
    return pl.pallas_call(
        body,
        in_specs=specs + [ANY] * len(after),
        out_specs=[VMEM] * len(shapes),
        out_shape=shapes,
        scratch_shapes=list(scratch),
        compiler_params=pltpu.CompilerParams(vmem_limit_bytes=limit << 20),
        cost_estimate=pl.CostEstimate(
            flops=int((time or TIMES[name]) * 1.15e9), bytes_accessed=0, transcendentals=0
        ),
        name=name,
    )(*args, *after)


def cut_body(axis, pieces, parts, count, *refs):
    sources, outs, sem = refs[:count], refs[-1 - count * len(parts) * len(pieces) : -1], refs[-1]
    copies = []
    core = core_index()
    for source in sources:
        for part in parts:
            begin = (core if part == "own" else 1 - core) * HALF
            at = 0
            for size in pieces:
                if axis == 1:
                    place = source.at[:, pl.ds(pl.multiple_of(begin + at, 128), size)]
                else:
                    place = source.at[pl.ds(pl.multiple_of(begin, 128), HALF), pl.ds(at, size)]
                at += size
                n = len(copies)
                copies.append(pltpu.make_async_copy(place, outs[n], sem.at[n]))
    for copy in copies:
        copy.start()
    for copy in copies:
        copy.wait()


def cut(axis, pieces, parts, weights, after=()):
    weights = [pltpu.with_memory_space_constraint(w, pltpu.HBM) for w in weights]
    rows = weights[0].shape[0] if axis == 1 else HALF
    shapes = [pltpu.VMEM((rows, size), BF) for size in pieces] * (len(parts) * len(weights))
    out = kernel(
        functools.partial(cut_body, axis, pieces, parts, len(weights)),
        "cut",
        weights,
        shapes,
        after,
        [pltpu.SemaphoreType.DMA((len(shapes),))],
        specs=[pl.BlockSpec(memory_space=pltpu.HBM)] * len(weights),
        time=5.0 * len(weights) * len(parts),
    )
    return [out[i : i + len(pieces)] for i in range(0, len(out), len(pieces))]


def hold_body(source, *refs):
    out, sem = refs[-2:]
    copy = pltpu.make_async_copy(source, out, sem)
    copy.start()
    copy.wait()


def hold(tokens, after):
    return kernel(
        hold_body,
        "stack",
        (pltpu.with_memory_space_constraint(tokens, pltpu.HBM),),
        [pltpu.VMEM(tokens.shape, BF)],
        after,
        [pltpu.SemaphoreType.DMA],
        specs=[pl.BlockSpec(memory_space=pltpu.HBM)],
    )[0]


def project_body(flow, sizes, *refs):
    count = 2 * len(sizes)
    blocks = refs[:count]
    weights = (refs[count : count + 2], refs[count + 2 : count + 4])
    send, keep, plain, turned = refs[-4:]
    pairs = sum(sizes)
    mask = mask_of(flow)
    at = 0
    for i, size in enumerate(sizes):
        for t in range(size):
            plain[pl.ds(at, 128)] = blocks[2 * i][t]
            plain[pl.ds(at + 128, 128)] = blocks[2 * i + 1][t]
            at += 256
    for t in range(pairs):
        for r in range(16):
            source = pl.multiple_of(t * 256 + (r ^ mask) * 16, 16)
            turned[pl.ds(t * 256 + r * 16, 16)] = plain[pl.ds(source, 16)]

    def store(k, columns, part):
        for t in range(pairs):
            send[k, t, :, columns] = part[t * 256 : t * 256 + 128]
            keep[k, t, :, columns] = part[t * 256 + 128 : t * 256 + 256]

    def multiply(weight):
        return jnp.dot(turned[...], weight, preferred_element_type=F32).astype(BF)

    for piece, base in ((0, 0), (1, WIDE[0])):
        for k in range(2):
            for at in range(0, 768, 256):
                part = multiply(weights[k][piece][:, at : at + 256])
                store(k, pl.ds(base + at, 256), part)
    both = jnp.concatenate((weights[0][0][:, 768:], weights[1][0][:, 768:]), axis=1)
    res = multiply(both)
    for k in range(2):
        store(k, pl.ds(768, 128), res[:, k * 128 : (k + 1) * 128])


def project(flow, tokens, gate, up, after=()):
    sizes = [mine.shape[0] for mine, _ in tokens]
    blocks = [block for both in tokens for block in both]
    rows = 256 * sum(sizes)
    shape = jax.ShapeDtypeStruct((2, sum(sizes), 128, HALF), BF)
    return kernel(
        functools.partial(project_body, flow, sizes),
        "project",
        (*blocks, *gate, *up),
        [shape] * 2,
        after,
        [pltpu.VMEM((rows, 1024), BF)] * 2,
        8,
        time=1.0,
    )


def down_body(flow, kind, t, count, *refs):
    rows, pieces, refs = refs[:count], refs[count : count + 2], refs[count + 2 :]
    mask = mask_of(flow)
    blocks = [block[i] for block in rows for i in range(block.shape[0])]
    left = jnp.concatenate(blocks, axis=0) if len(blocks) > 1 else blocks[0]
    for j in range(4):
        columns = pl.ds(j * 256, 256)
        weight = pieces[j // 2][:, j % 2 * 256 : (j % 2 + 1) * 256]
        res = jnp.dot(left, weight, preferred_element_type=F32)
        if kind == "half":
            refs[-1][:, columns] = res
            continue
        for i in range(len(blocks)):
            base = (t + i) * 128
            for r in range(16):
                spot = pl.ds(pl.multiple_of((r ^ mask) * 16, 16), 16)
                if r < 8:
                    value = res[i * 128 + r * 16 : i * 128 + (r + 1) * 16]
                else:
                    value = refs[0][pl.ds(base + (r - 8) * 16, 16), columns]
                refs[-1][i, spot, columns] = value
    if kind == "last":
        send, keep, total = refs[-3:]
        keep[...] = total[0, :128] + refs[1][t, :128]
        send[...] = (total[0, 128:] + refs[1][t, 128:]).astype(BF)


def down(flow, kind, rows, weights, extra=(), t=0, after=()):
    if kind == "half":
        shapes = [jax.ShapeDtypeStruct((256, 1024), F32)]
    elif kind == "last":
        shapes = [jax.ShapeDtypeStruct((128, 1024), BF), jax.ShapeDtypeStruct((128, 1024), F32)]
    else:
        shapes = [jax.ShapeDtypeStruct((2, 256, 1024), F32)]
    out = kernel(
        functools.partial(down_body, flow, kind, t, len(rows)),
        "down",
        (*rows, *weights, *extra),
        shapes,
        after,
        [pltpu.VMEM((1, 256, 1024), F32)] if kind == "last" else (),
        limit=4,
    )
    return out if kind == "last" else out[0]


def halves_body(before, keep, came, *refs):
    send, kept = refs[-2:]
    half = kept.shape[2]
    at = 0
    if before:
        old_send, old_kept = refs[:2]
        at = old_send.shape[1]
        send[:, :at] = old_send[...]
        kept[:, :at] = old_kept[...]
    for k in range(2):
        for t in range(keep.shape[1]):
            total = keep[k, t].astype(F32) + came[k, t].astype(F32)
            send[k, at + t] = total[:half].astype(BF)
            kept[k, at + t] = total[half:].astype(BF)


def halves(keep, came, done=(), after=()):
    spans = keep.shape[1] + (done[0].shape[1] if done else 0)
    shape = jax.ShapeDtypeStruct((2, spans, keep.shape[2] // 2, HALF), BF)
    body = functools.partial(halves_body, bool(done))
    return kernel(body, "halves", (keep, came, *done), [shape] * 2, after)


def add_body(keep, came, *refs):
    refs[-1][...] = (keep[...].astype(F32) + came[...].astype(F32)).astype(BF)


def add(keep, came, after):
    return kernel(add_body, "halves", (keep, came), [jax.ShapeDtypeStruct(keep.shape, BF)], after)[0]


def hidden_body(mine, theirs, *refs):
    half = mine.shape[2] // 2
    for at, other in ((0, half), (half, 0)):
        gate = mine[0, :, at : at + half].astype(F32) + theirs[0, :, other : other + half].astype(F32)
        up = mine[1, :, at : at + half].astype(F32) + theirs[1, :, other : other + half].astype(F32)
        refs[-1][:, at : at + half] = (gate / (1.0 + jnp.exp(-gate)) * up).astype(BF)


def hidden(mine, theirs, after):
    shape = jax.ShapeDtypeStruct(mine.shape[1:], BF)
    return kernel(hidden_body, "hidden", (mine, theirs), [shape], after)[0]


def join_body(count, theirs, mine, *refs):
    rows = mine.shape[1]
    each = 2 // count
    for i, out in enumerate(refs[-count:]):
        out[:, :rows] = theirs[i * each : (i + 1) * each]
        out[:, rows:] = mine[i * each : (i + 1) * each]


def join(theirs, mine, count=1, after=()):
    shape = jax.ShapeDtypeStruct((2 // count, 2 * mine.shape[1], HALF), BF)
    body = functools.partial(join_body, count)
    return kernel(body, "join", (theirs, mine), [shape] * count, after)


def stack_body(first, second, *refs):
    refs[-1][0] = first[...]
    refs[-1][1] = second[...]


def stack(first, second, after):
    shape = jax.ShapeDtypeStruct((2, *first.shape), BF)
    return kernel(stack_body, "stack", (first, second), [shape], after)[0]


class Line:
    def __init__(self):
        self.last = ()

    def __call__(self, call, *args):
        out = call(*args, after=self.last)
        first = out
        while isinstance(first, (list, tuple)):
            first = first[0]
        self.last = (first,)
        return out


TURNS = "ogj1u02310w23012301230123012301012323012323"


def local(tokens, gate_weight, up_weight, down_weight):
    line = Line()
    after, before = shift(tokens, -1), shift(tokens, 1)
    beside, far = swap(tokens), shift(tokens, 2)
    line.last = (beside,)
    near = line(hold, tokens)
    far_beside = swap(far)
    pair_a = [(near[None], beside[None]), (far[None], far_beside[None])]
    sides = []
    own, other = {}, {}
    finished = {}

    def unit(u):
        flow = u % 2
        held = own if u < 2 else other
        groups = [sides] if flow else [pair_a]
        parts = []
        for group in groups:
            send, keep = line(project, flow, group, held["g"], held["u"])
            parts.append((keep, exchange(send, flow, 0)))
            yield
        done = ()
        for i, part in enumerate(parts):
            if i:
                yield
            done = line(halves, *part, done)
        send, keep = done
        came = exchange(send, flow, 1)
        yield
        send, keep = line(halves, keep, came)
        came = exchange(send, flow, 2)
        yield
        rows = line(add, keep, came)
        came = exchange(rows, flow, 3)
        yield
        rows = line(hidden, rows, came)
        theirs = exchange(rows, flow, 2)
        yield
        (rows,) = line(join, theirs, rows)
        theirs = exchange(rows, flow, 1)
        yield
        rows = line(join, theirs, rows, 1 if u < 2 else 2)
        theirs = [exchange(part, flow, 0) for part in rows[::-1]]
        yield
        half = line(down, flow, "half", rows, held["w"])
        yield
        if u < 2:
            finished[u] = line(down, flow, "all", theirs, held["w"], (half,))
            yield
            return
        before = finished[u - 2]
        for t in (1, 0):
            part = line(down, flow, "last", [theirs[1 - t]], held["w"], (half, before), t)
            send, keep = part
            finished[u, t] = keep + swap(send).astype(F32)
            yield

    units = [unit(u) for u in range(4)]
    for turn in TURNS:
        if turn == "o":
            own["g"], own["u"] = line(cut, 1, WIDE, ("own",), (gate_weight, up_weight))
        elif turn in "gu":
            weight = gate_weight if turn == "g" else up_weight
            (given,) = line(cut, 1, WIDE, ("other",), (weight,))
            other[turn] = [swap(piece) for piece in given]
        elif turn == "w":
            own["w"], given = line(cut, 0, DOWN, ("own", "other"), (down_weight,))
            other["w"] = [swap(piece) for piece in given]
        elif turn == "j":
            both = line(stack, after, before)
            sides.append((both, swap(both)))
        else:
            next(units[int(turn)])

    from_opposite = shift(finished[2, 1].astype(BF), 2)
    from_after = shift(finished[3, 1].astype(BF), -1)
    from_before = shift(finished[3, 0].astype(BF), 1)
    total = finished[2, 0] + from_opposite.astype(F32)
    total = total + from_after.astype(F32) + from_before.astype(F32)
    return total.astype(BF)


def solution(mesh):
    placed = (P("group", "mp"), P("mp", "group"), P("mp", "group"), P("group", "mp"))
    return jax.shard_map(
        local, mesh=mesh, in_specs=placed, out_specs=P("group", "mp"), check_vma=False
    )
```

```python
import functools

import jax
import jax.numpy as jnp
from jax import lax
from jax.experimental import pallas as pl
from jax.experimental.pallas import tpu as pltpu
from jax.sharding import PartitionSpec as P

BF = jnp.bfloat16
F32 = jnp.float32

TIMES = {
    "down": 0.4,
    "halves": 2.0,
    "hidden": 2.0,
    "join": 2.0,
    "stack": 0.1,
}

PAIR = {"e": (1, 0, 3, 2), "o": (3, 2, 1, 0)}
ORDERS = (
    (("x", "e"), ("x", "o"), ("y", "e"), ("y", "o")),
    (("x", "o"), ("x", "e"), ("y", "o"), ("y", "e")),
), (
    (("y", "e"), ("y", "o"), ("x", "e"), ("x", "o")),
    (("y", "o"), ("y", "e"), ("x", "o"), ("x", "e")),
)
SWAP = [(g, g ^ 1) for g in range(8)]

HALF = 1664
WIDE = (896, 768)
DOWN = (512, 512)

VMEM = pl.BlockSpec(memory_space=pltpu.VMEM)
ANY = pl.BlockSpec(memory_space=pl.ANY)


def partner(m, link):
    axis, kind = link
    x, y = divmod(m, 4)
    return 4 * PAIR[kind][x] + y if axis == "x" else 4 * x + PAIR[kind][y]


def exchange(a, flow, step):
    pairs = [
        (g * 16 + m, g * 16 + partner(m, ORDERS[g % 2][flow][step]))
        for g in range(8)
        for m in range(16)
    ]
    return lax.ppermute(a, ("group", "mp"), pairs)


def swap(a):
    return lax.ppermute(a, "group", SWAP)


def shift(a, chips):
    return lax.ppermute(a, "group", [(g, (g + 2 * chips) % 8) for g in range(8)])


def core_index():
    return lax.axis_index("group") & 1


def mask_of(flow):
    place = lax.axis_index("mp")
    x, y = place >> 2, place & 3
    lead = x + core_index() * (y - x)
    rest = x + y - lead
    own = 0
    for at in (lead, rest):
        even, odd = ((at + 1) >> 1) & 1, at >> 1
        own = own * 4 + (2 * even + odd if flow == 0 else 2 * odd + even)
    return 15 ^ own


def kernel(body, name, args, shapes, after, scratch=(), limit=2, specs=None, time=None):
    specs = specs or [VMEM] * len(args)
    return pl.pallas_call(
        body,
        in_specs=specs + [ANY] * len(after),
        out_specs=[VMEM] * len(shapes),
        out_shape=shapes,
        scratch_shapes=list(scratch),
        compiler_params=pltpu.CompilerParams(vmem_limit_bytes=limit << 20),
        cost_estimate=pl.CostEstimate(
            flops=int((time or TIMES[name]) * 1.15e9), bytes_accessed=0, transcendentals=0
        ),
        name=name,
    )(*args, *after)


def cut_body(axis, pieces, parts, count, *refs):
    sources, outs, sem = refs[:count], refs[-1 - count * len(parts) * len(pieces) : -1], refs[-1]
    copies = []
    core = core_index()
    for source in sources:
        for part in parts:
            begin = (core if part == "own" else 1 - core) * HALF
            at = 0
            for size in pieces:
                if axis == 1:
                    place = source.at[:, pl.ds(pl.multiple_of(begin + at, 128), size)]
                else:
                    place = source.at[pl.ds(pl.multiple_of(begin, 128), HALF), pl.ds(at, size)]
                at += size
                n = len(copies)
                copies.append(pltpu.make_async_copy(place, outs[n], sem.at[n]))
    for copy in copies:
        copy.start()
    for copy in copies:
        copy.wait()


def cut(axis, pieces, parts, weights, after=()):
    weights = [pltpu.with_memory_space_constraint(w, pltpu.HBM) for w in weights]
    rows = weights[0].shape[0] if axis == 1 else HALF
    shapes = [pltpu.VMEM((rows, size), BF) for size in pieces] * (len(parts) * len(weights))
    out = kernel(
        functools.partial(cut_body, axis, pieces, parts, len(weights)),
        "cut",
        weights,
        shapes,
        after,
        [pltpu.SemaphoreType.DMA((len(shapes),))],
        specs=[pl.BlockSpec(memory_space=pltpu.HBM)] * len(weights),
        time=5.0 * len(weights) * len(parts),
    )
    return [out[i : i + len(pieces)] for i in range(0, len(out), len(pieces))]


def hold_body(source, *refs):
    out, sem = refs[-2:]
    copy = pltpu.make_async_copy(source, out, sem)
    copy.start()
    copy.wait()


def hold(tokens, after):
    return kernel(
        hold_body,
        "stack",
        (pltpu.with_memory_space_constraint(tokens, pltpu.HBM),),
        [pltpu.VMEM(tokens.shape, BF)],
        after,
        [pltpu.SemaphoreType.DMA],
        specs=[pl.BlockSpec(memory_space=pltpu.HBM)],
    )[0]


def project_body(flow, sizes, *refs):
    count = 2 * len(sizes)
    blocks = refs[:count]
    weights = (refs[count : count + 2], refs[count + 2 : count + 4])
    send, keep, plain, turned = refs[-4:]
    pairs = sum(sizes)
    mask = mask_of(flow)
    at = 0
    for i, size in enumerate(sizes):
        for t in range(size):
            plain[pl.ds(at, 128)] = blocks[2 * i][t]
            plain[pl.ds(at + 128, 128)] = blocks[2 * i + 1][t]
            at += 256
    for t in range(pairs):
        for r in range(16):
            source = pl.multiple_of(t * 256 + (r ^ mask) * 16, 16)
            turned[pl.ds(t * 256 + r * 16, 16)] = plain[pl.ds(source, 16)]

    def store(k, columns, part):
        for t in range(pairs):
            send[k, t, :, columns] = part[t * 256 : t * 256 + 128]
            keep[k, t, :, columns] = part[t * 256 + 128 : t * 256 + 256]

    def multiply(weight):
        return jnp.dot(turned[...], weight, preferred_element_type=F32).astype(BF)

    for piece, base in ((0, 0), (1, WIDE[0])):
        for k in range(2):
            for at in range(0, 768, 256):
                part = multiply(weights[k][piece][:, at : at + 256])
                store(k, pl.ds(base + at, 256), part)
    both = jnp.concatenate((weights[0][0][:, 768:], weights[1][0][:, 768:]), axis=1)
    res = multiply(both)
    for k in range(2):
        store(k, pl.ds(768, 128), res[:, k * 128 : (k + 1) * 128])


def project(flow, tokens, gate, up, after=()):
    sizes = [mine.shape[0] for mine, _ in tokens]
    blocks = [block for both in tokens for block in both]
    rows = 256 * sum(sizes)
    shape = jax.ShapeDtypeStruct((2, sum(sizes), 128, HALF), BF)
    return kernel(
        functools.partial(project_body, flow, sizes),
        "project",
        (*blocks, *gate, *up),
        [shape] * 2,
        after,
        [pltpu.VMEM((rows, 1024), BF)] * 2,
        8,
        time=1.0,
    )


def down_body(flow, kind, t, count, *refs):
    rows, pieces, refs = refs[:count], refs[count : count + 2], refs[count + 2 :]
    mask = mask_of(flow)
    blocks = [block[i] for block in rows for i in range(block.shape[0])]
    left = jnp.concatenate(blocks, axis=0) if len(blocks) > 1 else blocks[0]
    for j in range(4):
        columns = pl.ds(j * 256, 256)
        weight = pieces[j // 2][:, j % 2 * 256 : (j % 2 + 1) * 256]
        res = jnp.dot(left, weight, preferred_element_type=F32)
        if kind == "half":
            refs[-1][:, columns] = res
            continue
        for i in range(len(blocks)):
            base = (t + i) * 128
            for r in range(16):
                spot = pl.ds(pl.multiple_of((r ^ mask) * 16, 16), 16)
                if r < 8:
                    value = res[i * 128 + r * 16 : i * 128 + (r + 1) * 16]
                else:
                    value = refs[0][pl.ds(base + (r - 8) * 16, 16), columns]
                refs[-1][i, spot, columns] = value
    if kind == "last":
        send, keep, total = refs[-3:]
        keep[...] = total[0, :128] + refs[1][t, :128]
        send[...] = (total[0, 128:] + refs[1][t, 128:]).astype(BF)


def down(flow, kind, rows, weights, extra=(), t=0, after=()):
    if kind == "half":
        shapes = [jax.ShapeDtypeStruct((256, 1024), F32)]
    elif kind == "last":
        shapes = [jax.ShapeDtypeStruct((128, 1024), BF), jax.ShapeDtypeStruct((128, 1024), F32)]
    else:
        shapes = [jax.ShapeDtypeStruct((2, 256, 1024), F32)]
    out = kernel(
        functools.partial(down_body, flow, kind, t, len(rows)),
        "down",
        (*rows, *weights, *extra),
        shapes,
        after,
        [pltpu.VMEM((1, 256, 1024), F32)] if kind == "last" else (),
        limit=4,
    )
    return out if kind == "last" else out[0]


def halves_body(before, keep, came, *refs):
    send, kept = refs[-2:]
    half = kept.shape[2]
    at = 0
    if before:
        old_send, old_kept = refs[:2]
        at = old_send.shape[1]
        send[:, :at] = old_send[...]
        kept[:, :at] = old_kept[...]
    for k in range(2):
        for t in range(keep.shape[1]):
            total = keep[k, t].astype(F32) + came[k, t].astype(F32)
            send[k, at + t] = total[:half].astype(BF)
            kept[k, at + t] = total[half:].astype(BF)


def halves(keep, came, done=(), after=()):
    spans = keep.shape[1] + (done[0].shape[1] if done else 0)
    shape = jax.ShapeDtypeStruct((2, spans, keep.shape[2] // 2, HALF), BF)
    body = functools.partial(halves_body, bool(done))
    return kernel(body, "halves", (keep, came, *done), [shape] * 2, after)


def add_body(keep, came, *refs):
    refs[-1][...] = (keep[...].astype(F32) + came[...].astype(F32)).astype(BF)


def add(keep, came, after):
    return kernel(add_body, "halves", (keep, came), [jax.ShapeDtypeStruct(keep.shape, BF)], after)[0]


def hidden_body(mine, theirs, *refs):
    half = mine.shape[2] // 2
    for at, other in ((0, half), (half, 0)):
        gate = mine[0, :, at : at + half].astype(F32) + theirs[0, :, other : other + half].astype(F32)
        up = mine[1, :, at : at + half].astype(F32) + theirs[1, :, other : other + half].astype(F32)
        refs[-1][:, at : at + half] = (gate / (1.0 + jnp.exp(-gate)) * up).astype(BF)


def hidden(mine, theirs, after):
    shape = jax.ShapeDtypeStruct(mine.shape[1:], BF)
    return kernel(hidden_body, "hidden", (mine, theirs), [shape], after)[0]


def join_body(count, theirs, mine, *refs):
    rows = mine.shape[1]
    each = 2 // count
    for i, out in enumerate(refs[-count:]):
        out[:, :rows] = theirs[i * each : (i + 1) * each]
        out[:, rows:] = mine[i * each : (i + 1) * each]


def join(theirs, mine, count=1, after=()):
    shape = jax.ShapeDtypeStruct((2 // count, 2 * mine.shape[1], HALF), BF)
    body = functools.partial(join_body, count)
    return kernel(body, "join", (theirs, mine), [shape] * count, after)


def stack_body(first, second, *refs):
    refs[-1][0] = first[...]
    refs[-1][1] = second[...]


def stack(first, second, after):
    shape = jax.ShapeDtypeStruct((2, *first.shape), BF)
    return kernel(stack_body, "stack", (first, second), [shape], after)[0]


def keep_rows(rows, after):
    body = lambda source, *refs: refs[-1].__setitem__(..., source[...])
    return kernel(body, "stack", (rows,), [jax.ShapeDtypeStruct(rows.shape, BF)], after)[0]


class Line:
    def __init__(self):
        self.last = ()

    def __call__(self, call, *args):
        out = call(*args, after=self.last)
        first = out
        while isinstance(first, (list, tuple)):
            first = first[0]
        self.last = (first,)
        return out


TURNS = "ogju1k03120w32103210321032103210103232103232"


def local(tokens, gate_weight, up_weight, down_weight):
    line = Line()
    after, before = shift(tokens, -1), shift(tokens, 1)
    beside, far = swap(tokens), shift(tokens, 2)
    line.last = (beside,)
    near = line(hold, tokens)
    pair_a = [(near[None], beside[None])]
    sides = []
    own, other = {}, {}
    finished = {}

    def unit(u):
        flow = u % 2
        held = own if u < 2 else other
        groups = [sides] if flow else [pair_a]
        parts = []
        for group in groups:
            send, keep = line(project, flow, group, held["g"], held["u"])
            parts.append((keep, exchange(send, flow, 0)))
            yield
        done = ()
        for i, part in enumerate(parts):
            if i:
                yield
            done = line(halves, *part, done)
        send, keep = done
        came = exchange(send, flow, 1)
        yield
        send, keep = line(halves, keep, came)
        came = exchange(send, flow, 2)
        yield
        rows = line(add, keep, came)
        came = exchange(rows, flow, 3)
        yield
        rows = line(hidden, rows, came)
        theirs = exchange(rows, flow, 2)
        yield
        (rows,) = line(join, theirs, rows)
        theirs = exchange(rows, flow, 1)
        yield
        rows = line(join, theirs, rows, 1 if u < 2 else 2)
        theirs = [exchange(part, flow, 0) for part in rows[::-1]]
        yield
        half = line(down, flow, "half", rows, held["w"])
        yield
        if u < 2:
            finished[u] = line(down, flow, "all", theirs, held["w"], (half,))
            yield
            return
        before = finished[u - 2]
        for t in (1, 0):
            part = line(down, flow, "last", [theirs[1 - t]], held["w"], (half, before), t)
            send, keep = part
            finished[u, t] = keep + swap(send).astype(F32)
            yield

    units = [unit(u) for u in range(4)]
    for turn in TURNS:
        if turn == "o":
            own["g"], own["u"] = line(cut, 1, WIDE, ("own",), (gate_weight, up_weight))
        elif turn in "gu":
            weight = gate_weight if turn == "g" else up_weight
            (given,) = line(cut, 1, WIDE, ("other",), (weight,))
            other[turn] = [swap(piece) for piece in given]
        elif turn == "w":
            own["w"], given = line(cut, 0, DOWN, ("own", "other"), (down_weight,))
            other["w"] = [swap(piece) for piece in given]
        elif turn == "k":
            held = line(keep_rows, far)
            pair_a.append((held[None], swap(held)[None]))
        elif turn == "j":
            both = line(stack, after, before)
            sides.append((both, swap(both)))
        else:
            next(units[int(turn)])

    from_opposite = shift(finished[2, 1].astype(BF), 2)
    from_after = shift(finished[3, 1].astype(BF), -1)
    from_before = shift(finished[3, 0].astype(BF), 1)
    total = finished[2, 0] + from_opposite.astype(F32)
    total = total + from_after.astype(F32) + from_before.astype(F32)
    return total.astype(BF)


def solution(mesh):
    placed = (P("group", "mp"), P("mp", "group"), P("mp", "group"), P("group", "mp"))
    return jax.shard_map(
        local, mesh=mesh, in_specs=placed, out_specs=P("group", "mp"), check_vma=False
    )
```

```python
import functools

import jax
import jax.numpy as jnp
from jax import lax
from jax.experimental import pallas as pl
from jax.experimental.pallas import tpu as pltpu
from jax.sharding import PartitionSpec as P

BF = jnp.bfloat16
F32 = jnp.float32

TIMES = {
    "down": 0.4,
    "halves": 2.0,
    "hidden": 2.0,
    "join": 2.0,
    "stack": 0.1,
}

PAIR = {"e": (1, 0, 3, 2), "o": (3, 2, 1, 0)}
ORDERS = (
    (("x", "e"), ("x", "o"), ("y", "e"), ("y", "o")),
    (("x", "o"), ("x", "e"), ("y", "o"), ("y", "e")),
), (
    (("y", "e"), ("y", "o"), ("x", "e"), ("x", "o")),
    (("y", "o"), ("y", "e"), ("x", "o"), ("x", "e")),
)
SWAP = [(g, g ^ 1) for g in range(8)]

HALF = 1664
WIDE = (896, 768)
DOWN = (512, 512)

VMEM = pl.BlockSpec(memory_space=pltpu.VMEM)
ANY = pl.BlockSpec(memory_space=pl.ANY)


def partner(m, link):
    axis, kind = link
    x, y = divmod(m, 4)
    return 4 * PAIR[kind][x] + y if axis == "x" else 4 * x + PAIR[kind][y]


def exchange(a, flow, step):
    pairs = [
        (g * 16 + m, g * 16 + partner(m, ORDERS[g % 2][flow][step]))
        for g in range(8)
        for m in range(16)
    ]
    return lax.ppermute(a, ("group", "mp"), pairs)


def swap(a):
    return lax.ppermute(a, "group", SWAP)


def shift(a, chips):
    return lax.ppermute(a, "group", [(g, (g + 2 * chips) % 8) for g in range(8)])


def core_index():
    return lax.axis_index("group") & 1


def mask_of(flow):
    place = lax.axis_index("mp")
    x, y = place >> 2, place & 3
    lead = x + core_index() * (y - x)
    rest = x + y - lead
    own = 0
    for at in (lead, rest):
        even, odd = ((at + 1) >> 1) & 1, at >> 1
        own = own * 4 + (2 * even + odd if flow == 0 else 2 * odd + even)
    return 15 ^ own


def kernel(body, name, args, shapes, after, scratch=(), limit=2, specs=None, time=None):
    specs = specs or [VMEM] * len(args)
    return pl.pallas_call(
        body,
        in_specs=specs + [ANY] * len(after),
        out_specs=[VMEM] * len(shapes),
        out_shape=shapes,
        scratch_shapes=list(scratch),
        compiler_params=pltpu.CompilerParams(vmem_limit_bytes=limit << 20),
        cost_estimate=pl.CostEstimate(
            flops=int((time or TIMES[name]) * 1.15e9), bytes_accessed=0, transcendentals=0
        ),
        name=name,
    )(*args, *after)


def cut_body(axis, pieces, parts, count, *refs):
    sources, outs, sem = refs[:count], refs[-1 - count * len(parts) * len(pieces) : -1], refs[-1]
    copies = []
    core = core_index()
    for source in sources:
        for part in parts:
            begin = (core if part == "own" else 1 - core) * HALF
            at = 0
            for size in pieces:
                if axis == 1:
                    place = source.at[:, pl.ds(pl.multiple_of(begin + at, 128), size)]
                else:
                    place = source.at[pl.ds(pl.multiple_of(begin, 128), HALF), pl.ds(at, size)]
                at += size
                n = len(copies)
                copies.append(pltpu.make_async_copy(place, outs[n], sem.at[n]))
    for copy in copies:
        copy.start()
    for copy in copies:
        copy.wait()


def cut(axis, pieces, parts, weights, after=()):
    weights = [pltpu.with_memory_space_constraint(w, pltpu.HBM) for w in weights]
    rows = weights[0].shape[0] if axis == 1 else HALF
    shapes = [pltpu.VMEM((rows, size), BF) for size in pieces] * (len(parts) * len(weights))
    out = kernel(
        functools.partial(cut_body, axis, pieces, parts, len(weights)),
        "cut",
        weights,
        shapes,
        after,
        [pltpu.SemaphoreType.DMA((len(shapes),))],
        specs=[pl.BlockSpec(memory_space=pltpu.HBM)] * len(weights),
        time=5.0 * len(weights) * len(parts),
    )
    return [out[i : i + len(pieces)] for i in range(0, len(out), len(pieces))]


def hold_body(source, *refs):
    out, sem = refs[-2:]
    copy = pltpu.make_async_copy(source, out, sem)
    copy.start()
    copy.wait()


def hold(tokens, after):
    return kernel(
        hold_body,
        "stack",
        (pltpu.with_memory_space_constraint(tokens, pltpu.HBM),),
        [pltpu.VMEM(tokens.shape, BF)],
        after,
        [pltpu.SemaphoreType.DMA],
        specs=[pl.BlockSpec(memory_space=pltpu.HBM)],
    )[0]


def project_body(flow, sizes, *refs):
    count = 2 * len(sizes)
    blocks = refs[:count]
    weights = (refs[count : count + 2], refs[count + 2 : count + 4])
    send, keep, plain, turned = refs[-4:]
    pairs = sum(sizes)
    mask = mask_of(flow)
    at = 0
    for i, size in enumerate(sizes):
        for t in range(size):
            plain[pl.ds(at, 128)] = blocks[2 * i][t]
            plain[pl.ds(at + 128, 128)] = blocks[2 * i + 1][t]
            at += 256
    for t in range(pairs):
        for r in range(16):
            source = pl.multiple_of(t * 256 + (r ^ mask) * 16, 16)
            turned[pl.ds(t * 256 + r * 16, 16)] = plain[pl.ds(source, 16)]

    def store(k, columns, part):
        for t in range(pairs):
            send[k, t, :, columns] = part[t * 256 : t * 256 + 128]
            keep[k, t, :, columns] = part[t * 256 + 128 : t * 256 + 256]

    def multiply(weight):
        return jnp.dot(turned[...], weight, preferred_element_type=F32).astype(BF)

    for piece, base in ((0, 0), (1, WIDE[0])):
        for k in range(2):
            for at in range(0, 768, 256):
                part = multiply(weights[k][piece][:, at : at + 256])
                store(k, pl.ds(base + at, 256), part)
    both = jnp.concatenate((weights[0][0][:, 768:], weights[1][0][:, 768:]), axis=1)
    res = multiply(both)
    for k in range(2):
        store(k, pl.ds(768, 128), res[:, k * 128 : (k + 1) * 128])


def project(flow, tokens, gate, up, after=()):
    sizes = [mine.shape[0] for mine, _ in tokens]
    blocks = [block for both in tokens for block in both]
    rows = 256 * sum(sizes)
    shape = jax.ShapeDtypeStruct((2, sum(sizes), 128, HALF), BF)
    return kernel(
        functools.partial(project_body, flow, sizes),
        "project",
        (*blocks, *gate, *up),
        [shape] * 2,
        after,
        [pltpu.VMEM((rows, 1024), BF)] * 2,
        8,
        time=1.0,
    )


def down_body(flow, kind, t, count, *refs):
    rows, pieces, refs = refs[:count], refs[count : count + 2], refs[count + 2 :]
    mask = mask_of(flow)
    blocks = [block[i] for block in rows for i in range(block.shape[0])]
    left = jnp.concatenate(blocks, axis=0) if len(blocks) > 1 else blocks[0]
    for j in range(4):
        columns = pl.ds(j * 256, 256)
        weight = pieces[j // 2][:, j % 2 * 256 : (j % 2 + 1) * 256]
        res = jnp.dot(left, weight, preferred_element_type=F32)
        if kind == "half":
            refs[-1][:, columns] = res
            continue
        for i in range(len(blocks)):
            base = (t + i) * 128
            for r in range(16):
                spot = pl.ds(pl.multiple_of((r ^ mask) * 16, 16), 16)
                if r < 8:
                    value = res[i * 128 + r * 16 : i * 128 + (r + 1) * 16]
                else:
                    value = refs[0][pl.ds(base + (r - 8) * 16, 16), columns]
                refs[-1][i, spot, columns] = value
    if kind == "last":
        send, keep, total = refs[-3:]
        keep[...] = total[0, :128] + refs[1][t, :128]
        send[...] = (total[0, 128:] + refs[1][t, 128:]).astype(BF)


def down(flow, kind, rows, weights, extra=(), t=0, after=()):
    if kind == "half":
        shapes = [jax.ShapeDtypeStruct((256, 1024), F32)]
    elif kind == "last":
        shapes = [jax.ShapeDtypeStruct((128, 1024), BF), jax.ShapeDtypeStruct((128, 1024), F32)]
    else:
        shapes = [jax.ShapeDtypeStruct((2, 256, 1024), F32)]
    out = kernel(
        functools.partial(down_body, flow, kind, t, len(rows)),
        "down",
        (*rows, *weights, *extra),
        shapes,
        after,
        [pltpu.VMEM((1, 256, 1024), F32)] if kind == "last" else (),
        limit=4,
    )
    return out if kind == "last" else out[0]


def halves_body(before, keep, came, *refs):
    send, kept = refs[-2:]
    half = kept.shape[2]
    at = 0
    if before:
        old_send, old_kept = refs[:2]
        at = old_send.shape[1]
        send[:, :at] = old_send[...]
        kept[:, :at] = old_kept[...]
    for k in range(2):
        for t in range(keep.shape[1]):
            total = keep[k, t].astype(F32) + came[k, t].astype(F32)
            send[k, at + t] = total[:half].astype(BF)
            kept[k, at + t] = total[half:].astype(BF)


def halves(keep, came, done=(), after=()):
    spans = keep.shape[1] + (done[0].shape[1] if done else 0)
    shape = jax.ShapeDtypeStruct((2, spans, keep.shape[2] // 2, HALF), BF)
    body = functools.partial(halves_body, bool(done))
    return kernel(body, "halves", (keep, came, *done), [shape] * 2, after)


def add_body(keep, came, *refs):
    refs[-1][...] = (keep[...].astype(F32) + came[...].astype(F32)).astype(BF)


def add(keep, came, after):
    return kernel(add_body, "halves", (keep, came), [jax.ShapeDtypeStruct(keep.shape, BF)], after)[0]


def hidden_body(mine, theirs, *refs):
    half = mine.shape[2] // 2
    for at, other in ((0, half), (half, 0)):
        gate = mine[0, :, at : at + half].astype(F32) + theirs[0, :, other : other + half].astype(F32)
        up = mine[1, :, at : at + half].astype(F32) + theirs[1, :, other : other + half].astype(F32)
        refs[-1][:, at : at + half] = (gate / (1.0 + jnp.exp(-gate)) * up).astype(BF)


def hidden(mine, theirs, after):
    shape = jax.ShapeDtypeStruct(mine.shape[1:], BF)
    return kernel(hidden_body, "hidden", (mine, theirs), [shape], after)[0]


def join_body(count, theirs, mine, *refs):
    rows = mine.shape[1]
    each = 2 // count
    for i, out in enumerate(refs[-count:]):
        out[:, :rows] = theirs[i * each : (i + 1) * each]
        out[:, rows:] = mine[i * each : (i + 1) * each]


def join(theirs, mine, count=1, after=()):
    shape = jax.ShapeDtypeStruct((2 // count, 2 * mine.shape[1], HALF), BF)
    body = functools.partial(join_body, count)
    return kernel(body, "join", (theirs, mine), [shape] * count, after)


def stack_body(first, second, *refs):
    refs[-1][0] = first[...]
    refs[-1][1] = second[...]


def stack(first, second, after):
    shape = jax.ShapeDtypeStruct((2, *first.shape), BF)
    return kernel(stack_body, "stack", (first, second), [shape], after)[0]


def keep_rows(rows, after):
    body = lambda source, *refs: refs[-1].__setitem__(..., source[...])
    return kernel(body, "stack", (rows,), [jax.ShapeDtypeStruct(rows.shape, BF)], after)[0]


class Line:
    def __init__(self):
        self.last = ()

    def __call__(self, call, *args):
        out = call(*args, after=self.last)
        first = out
        while isinstance(first, (list, tuple)):
            first = first[0]
        self.last = (first,)
        return out


TURNS = "ogju1k03120w32103210321032103210321032103232"


def local(tokens, gate_weight, up_weight, down_weight):
    line = Line()
    after, before = shift(tokens, -1), shift(tokens, 1)
    beside, far = swap(tokens), shift(tokens, 2)
    line.last = (beside,)
    near = line(hold, tokens)
    pair_a = [(near[None], beside[None])]
    sides = []
    own, other = {}, {}
    finished = {}

    def unit(u):
        flow = u % 2
        held = own if u < 2 else other
        groups = [sides] if flow else [pair_a]
        parts = []
        for group in groups:
            send, keep = line(project, flow, group, held["g"], held["u"])
            parts.append((keep, exchange(send, flow, 0)))
            yield
        done = ()
        for i, part in enumerate(parts):
            if i:
                yield
            done = line(halves, *part, done)
        send, keep = done
        came = exchange(send, flow, 1)
        yield
        send, keep = line(halves, keep, came)
        came = exchange(send, flow, 2)
        yield
        rows = line(add, keep, came)
        came = exchange(rows, flow, 3)
        yield
        rows = line(hidden, rows, came)
        theirs = exchange(rows, flow, 2)
        yield
        (rows,) = line(join, theirs, rows)
        theirs = exchange(rows, flow, 1)
        yield
        rows = line(join, theirs, rows, 1 if u < 2 else 2)
        theirs = [exchange(part, flow, 0) for part in rows[::-1]]
        yield
        half = line(down, flow, "half", rows, held["w"])
        yield
        if u < 2:
            finished[u] = line(down, flow, "all", theirs, held["w"], (half,))
            yield
            return
        before = finished[u - 2]
        for t in (1, 0):
            part = line(down, flow, "last", [theirs[1 - t]], held["w"], (half, before), t)
            send, keep = part
            finished[u, t] = keep + swap(send).astype(F32)
            yield

    units = [unit(u) for u in range(4)]
    for turn in TURNS:
        if turn == "o":
            own["g"], own["u"] = line(cut, 1, WIDE, ("own",), (gate_weight, up_weight))
        elif turn in "gu":
            weight = gate_weight if turn == "g" else up_weight
            (given,) = line(cut, 1, WIDE, ("other",), (weight,))
            other[turn] = [swap(piece) for piece in given]
        elif turn == "w":
            own["w"], given = line(cut, 0, DOWN, ("own", "other"), (down_weight,))
            other["w"] = [swap(piece) for piece in given]
        elif turn == "k":
            held = line(keep_rows, far)
            pair_a.append((held[None], swap(held)[None]))
        elif turn == "j":
            both = line(stack, after, before)
            sides.append((both, swap(both)))
        else:
            next(units[int(turn)])

    from_opposite = shift(finished[2, 1].astype(BF), 2)
    from_after = shift(finished[3, 1].astype(BF), -1)
    from_before = shift(finished[3, 0].astype(BF), 1)
    total = finished[2, 0] + from_opposite.astype(F32)
    total = total + from_after.astype(F32) + from_before.astype(F32)
    return total.astype(BF)


def solution(mesh):
    placed = (P("group", "mp"), P("mp", "group"), P("mp", "group"), P("group", "mp"))
    return jax.shard_map(
        local, mesh=mesh, in_specs=placed, out_specs=P("group", "mp"), check_vma=False
    )
```
